512 devices in a mesh: prompt: 64 (over y, z), seq: 8 (over x, core).
Axes of the slice: x: 4, y: 8, z: 8, core: 2. Of those that a mesh axis runs over, the one named last changes fastest.
Arguments:
- beam_rows: bfloat16 [2, 4096, 5120], P(None, 'prompt', 'seq'), may hold values from -240 to 240
- route: int32 [2, 4096, 1], P(None, 'prompt'), may hold values from 0 to 63; in each aligned block of 64 rows (0 to 63, 64 to 127, ..., all dimensions but the last counted through in order) at most 2 rows name the same one
- parent: int32 [2, 4096], P(None, 'prompt'), may hold values from 0 to 31
- prefix_kv: bfloat16 [64, 1024, 1024], P('prompt', 'seq'), may hold values from -6 to 6
- pages: bfloat16 [2048, 128, 1024], P('prompt', 'seq'), may hold values from -6 to 6
Outputs:
- attended: bfloat16 [2, 4096, 4096], P(None, 'prompt', 'seq')
The draws below stay inside these ranges and needn't reach their ends.
Inputs may be any that keep to these rules, and one draw needn't show every extreme that they name: `route`: in each step, among the 64 rows of one device along prompt at most 2 name the same prompt. `parent`: index of a page among the 32 pages held by the same index of prompt as the row.
All inputs are finite; a program needn't handle non-finite values.
Results may differ from the reference program's by a relative error of at most 0.0042.
Values may be sent and summed in bfloat16 or wider, within the bound.
No kernel may reach another device: no remote copies, remote signals or barrier semaphores. Data moves between devices by JAX's collectives and lax.ppermute only.
A program may use at most 128 MiB of HBM per device.

```python
import math
import jax
import jax.numpy as jnp
import numpy as np
from jax import lax

HQ = 32
KVH = 4
DH = 128
PAGE = 128
STEPS = 2
PRE_DEV = 128
ROW_DEV = 64
PAGES_DEV = 32
PRE = 1024
PSEG = 16
ROWS = 4096
CAP = 2
FEAT = 5120
N_PROMPT = 64
N_SEQ = 8


def draw_beam_rows(key, part):
    key = jax.random.fold_in(key, 7)
    first = jax.random.fold_in(key, 0)
    values = jnp.clip(jax.random.normal(first, (STEPS, ROWS, FEAT), jnp.float32), -6.0, 6.0)
    return values.astype(jnp.bfloat16)


def touch_ends(entries, rng, smallest, top_value):
    shape = entries.shape
    spot = [jax.random.randint(jax.random.fold_in(rng, axis), (), 0, shape[axis]) for axis in range(len(shape))]
    entries = entries.at[tuple(spot)].set(smallest)
    longest = shape.index(max(shape))
    spot[longest] = (spot[longest] + 1) % shape[longest]
    return entries.at[tuple(spot)].set(top_value)


def steps_of(key, shape, cuts, least, top_value):
    level = 1.0
    for position, blocks in cuts:
        heights = jax.random.uniform(jax.random.fold_in(jax.random.fold_in(key, 6), position), (blocks,), jnp.float32, least / len(cuts), top_value / len(cuts))
        level = level * jnp.repeat(jnp.exp(heights), shape[position] // blocks).reshape((-1,) + (1,) * (len(shape) - 1 - position))
    return level


def shared_out(stream_key, own, number, rows, count, top, reach, skew):
    sequence = jax.random.permutation(stream_key, count)
    packed, ordinary = load_shares(count, rows * top, reach, skew, True), load_shares(count, rows * top, reach, skew, False)
    places = jnp.arange(count)

    def named(tallies, rotation):
        used = int((tallies > 0).sum())
        fixed = max(1, used // 4)
        shifted = fixed + (places - fixed + rotation * (used - fixed)) % max(1, count - fixed)
        return jnp.zeros((count,), jnp.int32).at[sequence[jnp.where(places < fixed, places, shifted)]].set(jnp.asarray(tallies, jnp.int32))

    tallies = jnp.where(number % 4 == 0, named(packed, number // 4), named(ordinary, number - number // 4 - 1))
    mixed = jax.random.permutation(jax.random.fold_in(own, 3), count)
    donor, receiver = mixed[0:count // 2 * 2:2], mixed[1:count // 2 * 2:2]
    room = jnp.minimum(tallies[donor] - 1, reach - tallies[receiver]) // 2
    room = jnp.where((donor == sequence[0]) | (receiver == sequence[0]) | (tallies[receiver] == 0), 0, jnp.maximum(room, 0))
    shifted = jax.random.randint(jax.random.fold_in(own, 4), (count // 2,), 0, 1 << 20) % (room + 1)
    tallies = tallies.at[donor].add(-shifted).at[receiver].add(shifted)
    labels = jnp.searchsorted(jnp.cumsum(tallies), jnp.arange(rows * top), side="right").astype(jnp.int32)
    listing = labels.reshape(top, rows).T
    listing = listing[jax.random.permutation(jax.random.fold_in(own, 1), rows)]
    rotation = jax.random.randint(jax.random.fold_in(own, 2), (rows, 1), 0, top)
    return jnp.take_along_axis(listing, (jnp.arange(top)[None, :] + rotation) % top, axis=1)


def load_shares(number_of, total, bound, slope, full):
    portions = [(1 << 20) // math.isqrt(rank ** slope) + 1 for rank in range(1, number_of + 1)]
    largest = bound if full else min(bound, max(-(-total // number_of), total * portions[0] // sum(portions)))
    least = 1 if total - largest >= number_of - 1 else 0
    given, spare = [largest] + [least] * (number_of - 1), total - largest - least * (number_of - 1)
    while spare > 0:
        movable = [i for i in range(1, number_of) if given[i] < largest] or [i for i in range(1, number_of) if given[i] < bound]
        pool, left = sum([portions[i] for i in movable]), spare
        for i in movable:
            addition = min(bound - given[i], max(1, left * portions[i] // pool), spare)
            given[i] = given[i] + addition
            spare = spare - addition
    return np.array(given)


def gaussian(key, shape, spread, most, cuts=(), kind=jnp.bfloat16):
    drawn = spread * jax.random.normal(key, shape, jnp.float32)
    if cuts:
        drawn = drawn * steps_of(key, shape, cuts, -0.22, 0.18)
    return jnp.clip(drawn, -most, most).astype(kind)


def setup_inputs(seed: int = 0) -> dict:
    seeds = jax.random.split(jax.random.key(seed), 6)
    beam_rows = draw_beam_rows(jax.random.fold_in(seeds[5], 71), 0)
    route_keys = jax.random.split(jax.random.fold_in(seeds[1], 1), STEPS * ROWS // ROW_DEV)
    route_turns = jax.random.permutation(jax.random.fold_in(seeds[1], 3), STEPS * ROWS // ROW_DEV)
    route = jax.vmap(lambda own, number: shared_out(jax.random.fold_in(seeds[1], 2), own, number, ROW_DEV, N_PROMPT, 1, CAP, 2))(route_keys, route_turns).reshape((STEPS, ROWS, 1))
    parent = touch_ends(jax.random.randint(seeds[2], (STEPS, ROWS), 0, PAGES_DEV), jax.random.fold_in(seeds[2], 1), 0, PAGES_DEV - 1).astype(jnp.int32)
    prefix_kv = gaussian(seeds[3], (N_PROMPT, PRE, 2 * KVH * DH), 1.0, 6.0, ((0, 64), (1, 8)))
    pages = gaussian(seeds[4], (N_PROMPT * PAGES_DEV, PAGE, 2 * KVH * DH), 1.0, 6.0, ((0, 64), (1, 8)))
    return {"beam_rows": beam_rows, "route": route, "parent": parent, "prefix_kv": prefix_kv, "pages": pages}


def block_stats(queries, block_rows):
    group_size = HQ // KVH
    score_scale = DH ** -0.5
    key_rows = block_rows[:, :KVH * DH].reshape(-1, KVH, DH).astype(jnp.float32)
    value_rows = block_rows[:, KVH * DH:].reshape(-1, KVH, DH).astype(jnp.float32)
    scores = jnp.einsum('kgd,tkd->kgt', queries.astype(jnp.float32), key_rows) * score_scale
    highest = jnp.max(scores, axis=-1)
    weights = jnp.exp(scores - highest[..., None]).astype(jnp.bfloat16)
    weights = lax.optimization_barrier(weights).astype(jnp.float32)
    totals = jnp.sum(weights, axis=-1)
    partial_sum = jnp.einsum('kgt,tkd->kgd', weights, value_rows)
    return highest, totals, partial_sum


def attend_row(beam_row, prompt_id, page_id, prefix_kv, pages):
    group_size = HQ // KVH
    score_scale = DH ** -0.5
    queries = beam_row[:HQ * DH].reshape(KVH, group_size, DH)
    own_key = beam_row[HQ * DH:HQ * DH + KVH * DH].reshape(KVH, DH).astype(jnp.float32)
    own_value = beam_row[HQ * DH + KVH * DH:].reshape(KVH, DH).astype(jnp.float32)
    prefix_rows = lax.dynamic_index_in_dim(prefix_kv, prompt_id, 0, keepdims=False)
    prefix_blocks = prefix_rows.reshape(N_SEQ, PRE_DEV, 2 * KVH * DH)
    page_rows = lax.dynamic_index_in_dim(pages, page_id, 0, keepdims=False)
    page_blocks = page_rows.reshape(N_SEQ, PSEG, 2 * KVH * DH)
    high_pre, sum_pre, val_pre = jax.vmap(block_stats, (None, 0))(queries, prefix_blocks)
    high_page, sum_page, val_page = jax.vmap(block_stats, (None, 0))(queries, page_blocks)
    own_score = jnp.einsum('kgd,kd->kg', queries.astype(jnp.float32), own_key) * score_scale
    own_val = jnp.broadcast_to(own_value[:, None, :], (KVH, group_size, DH))
    high_all = jnp.concatenate([high_pre, high_page, own_score[None]], axis=0)
    sum_all = jnp.concatenate([sum_pre, sum_page, jnp.ones((1, KVH, group_size), jnp.float32)], axis=0)
    val_all = jnp.concatenate([val_pre, val_page, own_val[None]], axis=0)
    overall = jnp.max(high_all, axis=0)
    factor = jnp.exp(high_all - overall[None])
    denom = jnp.sum(sum_all * factor, axis=0)
    numer = jnp.sum(val_all * factor[..., None], axis=0)
    return (numer / denom[..., None]).reshape(HQ * DH).astype(jnp.bfloat16)


def reference(beam_rows, route, parent, prefix_kv, pages):
    block_size = 8
    results = []
    for step_index in range(STEPS):
        row_ids = jnp.arange(ROWS, dtype=jnp.int32)
        page_ids = (row_ids // ROW_DEV) * PAGES_DEV + parent[step_index]
        prompt_ids = route[step_index, :, 0]
        grouped = (beam_rows[step_index].reshape(ROWS // block_size, block_size, FEAT),
                   prompt_ids.reshape(ROWS // block_size, block_size),
                   page_ids.reshape(ROWS // block_size, block_size))

        def run_block(items):
            return jax.vmap(attend_row, (0, 0, 0, None, None))(items[0], items[1], items[2], prefix_kv, pages)

        outcome = lax.map(run_block, grouped)
        results.append(outcome.reshape(ROWS, HQ * DH))
    return jnp.stack(results)
```

```python
import jax
import jax.numpy as jnp
from jax import lax
from jax.experimental import pallas as pl
from jax.experimental.pallas import tpu as pltpu
from jax.sharding import PartitionSpec as P

HQ = 32
KVH = 4
DH = 128
CAP = 2
SCALE = DH ** (-0.5)
BF = jnp.bfloat16
F32 = jnp.float32
NT = (((1,), (1,)), ((), ()))
NN = (((1,), (0,)), ((), ()))
TN = (((0,), (0,)), ((), ()))
VMEM = pl.BlockSpec(memory_space=pltpu.VMEM)
SMEM = pl.BlockSpec(memory_space=pltpu.SMEM)


def dot(a, b, dims):
    return lax.dot_general(a, b, dims, preferred_element_type=F32)


def call(kernel, outs, in_specs, scratch=(), flops=0, nbytes=0, name=None):
    return pl.pallas_call(
        kernel,
        out_shape=outs,
        in_specs=in_specs,
        out_specs=jax.tree.map(lambda _: VMEM, outs),
        scratch_shapes=list(scratch),
        compiler_params=pltpu.CompilerParams(vmem_limit_bytes=40 * 1024 * 1024),
        cost_estimate=pl.CostEstimate(flops=flops, bytes_accessed=nbytes, transcendentals=0),
        name=name,
    )


def slots_kernel(seq_ref, own_ref, near_ref, far_ref, rcol_ref, rrow_ref, sent_ref, query_ref, line):
    rows = own_ref.shape[0]
    width = own_ref.shape[1]
    half = rows // 2
    line[:, :width] = far_ref[...]
    line[:, width : 2 * width] = near_ref[...]
    line[:, 2 * width :] = own_ref[...]
    first = pl.multiple_of((10 - seq_ref[0]) * DH, DH)
    query = line[:, pl.ds(first, query_ref.shape[1])]
    query_ref[...] = query
    before = lax.broadcasted_iota(jnp.int32, (rows, rows), 0)
    after = lax.broadcasted_iota(jnp.int32, (rows, rows), 1)
    same = (rcol_ref[...] == rrow_ref[...]) & (before < after) & ((before < half) == (after < half))
    rank = jnp.sum(same.astype(jnp.int32), axis=0, keepdims=True)
    step = (lax.broadcasted_iota(jnp.int32, (1, rows), 1) >= half).astype(jnp.int32)
    position = rrow_ref[...] * (2 * CAP) + step * CAP + rank
    slot = lax.broadcasted_iota(jnp.int32, (sent_ref.shape[0], rows), 0)
    onehot = (slot == position).astype(F32).astype(BF)
    sent_ref[...] = dot(onehot, query, NN).astype(BF)


def thirds(value):
    high = value.astype(BF).astype(F32)
    rest = value - high
    middle = rest.astype(BF).astype(F32)
    low = (rest - middle).astype(BF).astype(F32)
    return [high, middle, low]


def prefix_kernel(query_ref, kv_ref, out_ref):
    slots = query_ref.shape[0]
    blocks = kv_ref.shape[0]
    heads = query_ref.shape[1] // DH
    values_t = [kv_ref[b, :, DH:].astype(F32).T.astype(BF) for b in range(blocks)]
    stats = []
    for h in range(heads):
        query = query_ref[:, h * DH : (h + 1) * DH]
        tops, totals, parts = [], [], []
        for b in range(blocks):
            scores = dot(kv_ref[b, :, :DH], query, NT) * SCALE
            top = jnp.max(scores, axis=0, keepdims=True)
            weights = jnp.exp(scores - top).astype(BF)
            tops.append(top)
            totals.append(jnp.sum(weights.astype(F32), axis=0, keepdims=True))
            parts.append(dot(values_t[b], weights, NN))
        top = tops[0]
        for b in range(1, blocks):
            top = jnp.maximum(top, tops[b])
        total = jnp.zeros_like(top)
        mixed = jnp.zeros((DH, slots), F32)
        for b in range(blocks):
            factor = jnp.exp(tops[b] - top)
            total += totals[b] * factor
            mixed += parts[b] * factor
        mixed = mixed / total
        out_ref[:, h * DH : (h + 1) * DH] = mixed.T.astype(BF)
        stats += thirds(top) + thirds(total) + [jnp.zeros_like(top)] * 2
    stats.append(jnp.zeros((DH - len(stats), slots), F32))
    out_ref[:, heads * DH :] = jnp.concatenate(stats, axis=0).T.astype(BF)


def page_kernel(seq_ref, query_ref, parent_ref, mine_ref, other_ref, out_ref, stat_ref):
    rows = query_ref.shape[0]
    heads = query_ref.shape[1] // DH
    senders = mine_ref.shape[0]
    page_rows = mine_ref.shape[1] - rows
    seg = DH // (2 * senders)
    page_count = page_rows // seg
    query = jnp.concatenate([query_ref[:, h * DH : (h + 1) * DH] for h in range(heads)], axis=0)
    parent = jnp.concatenate([parent_ref[...]] * heads, axis=1)

    def page(j, first):
        at = pl.ds(pl.multiple_of(j * seg, seg), seg)
        return jnp.concatenate(
            [ref[x, at, first : first + DH] for ref in (mine_ref, other_ref) for x in range(senders)], axis=0
        )

    def score(j, held):
        return jnp.where(parent == j, dot(page(j, 0), query, NT), held)

    scores = lax.fori_loop(0, page_count, score, jnp.zeros((DH, heads * rows), F32)) * SCALE
    top = jnp.max(scores, axis=0, keepdims=True)
    weights = jnp.exp(scores - top).astype(BF).astype(F32)
    total = jnp.sum(weights, axis=0, keepdims=True)

    def weigh(j, held):
        chosen = jnp.where(parent == j, weights, 0.0).astype(BF)
        return held + dot(page(j, DH), chosen, TN)

    mixed = lax.fori_loop(0, page_count, weigh, jnp.zeros((DH, heads * rows), F32))
    stats = [top[:, h * rows : (h + 1) * rows] for h in range(heads)]
    stats += [total[:, h * rows : (h + 1) * rows] for h in range(heads)]
    stats.append(jnp.zeros((DH - 2 * heads, rows), F32))
    stats = jnp.concatenate(stats, axis=0).T
    place = seq_ref[0]
    even_core = lax.rem(place, 2) == 0
    mine = mine_ref[senders - 1, page_rows:, :]
    other = other_ref[senders - 1, page_rows:, :]
    even = jnp.where(even_core, mine, other)
    odd = jnp.where(even_core, other, mine)
    own_key = jnp.where(place // 2 < senders - 1, even[:, :DH], odd[:, :DH]).astype(F32)
    own_value = odd[:, DH:].astype(F32)
    lane = lax.broadcasted_iota(jnp.int32, (rows, DH), 1)
    packed = jnp.zeros((rows, DH), F32)
    for h in range(heads):
        cols = slice(h * DH, (h + 1) * DH)
        own_score = jnp.sum(query_ref[:, cols].astype(F32) * own_key, axis=1, keepdims=True) * SCALE
        page_top = stats[:, h : h + 1]
        best = jnp.maximum(page_top, own_score)
        factor_page = jnp.exp(page_top - best)
        factor_own = jnp.exp(own_score - best)
        both = stats[:, heads + h : heads + h + 1] * factor_page + factor_own
        part = mixed[:, h * rows : (h + 1) * rows].T
        out_ref[:, cols] = part * factor_page + factor_own * own_value
        packed = jnp.where(lane == h, best, packed)
        packed = jnp.where(lane == heads + h, both, packed)
    stat_ref[...] = packed


def finish_kernel(back_ref, rcol_ref, rrow_ref, part_ref, stat_ref, out_ref):
    rows = part_ref.shape[0]
    half = rows // 2
    heads = part_ref.shape[1] // DH
    this = lax.broadcasted_iota(jnp.int32, (rows, rows), 0)
    before = lax.broadcasted_iota(jnp.int32, (rows, rows), 1)
    same = (rcol_ref[...] == rrow_ref[...]) & (before < this) & ((before < half) == (this < half))
    rank = jnp.sum(same.astype(jnp.int32), axis=1, keepdims=True)
    step = (lax.broadcasted_iota(jnp.int32, (rows, 1), 0) >= half).astype(jnp.int32)
    position = rcol_ref[...] * (2 * CAP) + step * CAP + rank
    slot = lax.broadcasted_iota(jnp.int32, (rows, back_ref.shape[0]), 1)
    onehot = (slot == position).astype(F32).astype(BF)
    got = dot(onehot, back_ref[...], NN)
    stats = stat_ref[...]
    for h in range(heads):
        cols = slice(h * DH, (h + 1) * DH)
        at = heads * DH + 8 * h
        prefix_top = got[:, at : at + 1] + got[:, at + 1 : at + 2] + got[:, at + 2 : at + 3]
        prefix_total = got[:, at + 3 : at + 4] + got[:, at + 4 : at + 5] + got[:, at + 5 : at + 6]
        home_top = stats[:, h : h + 1]
        home_total = stats[:, heads + h : heads + h + 1]
        best = jnp.maximum(prefix_top, home_top)
        factor_prefix = jnp.exp(prefix_top - best) * prefix_total
        factor_home = jnp.exp(home_top - best)
        denom = factor_prefix + home_total * factor_home
        numer = got[:, cols] * factor_prefix + part_ref[:, cols] * factor_home
        out_ref[:, cols] = (numer / denom).astype(BF)


def by_head(tokens):
    count = tokens.shape[0]
    return tokens.reshape(count, 2, KVH, DH).transpose(2, 0, 1, 3).reshape(KVH, count, 2 * DH)


def body(beam_rows, route, parent, prefix_kv, pages):
    prompt_count = lax.axis_size("prompt")
    seq_count = lax.axis_size("seq")
    step_count, row_count, width = beam_rows.shape
    rows = step_count * row_count
    head_part = HQ // seq_count
    out_width = head_part * DH
    slots = prompt_count * step_count * CAP
    place = lax.axis_index("seq").astype(jnp.int32).reshape(1)
    own = beam_rows.reshape(rows, width)
    route_col = route.reshape(rows, 1)
    route_row = route.reshape(1, rows)

    with jax.named_scope("rows_to_heads"):
        near = lax.ppermute(own, "seq", [(i, i + 1) for i in range(seq_count - 1)])
        far = lax.ppermute(own, "seq", [(4, 6), (5, 7)])
    with jax.named_scope("prefix_to_heads"):
        prefix = jnp.repeat(by_head(prefix_kv[0]), 2, axis=0)
        prefix = lax.all_to_all(prefix, "seq", 0, 0, tiled=True)
    with jax.named_scope("slots"):
        sent, query = call(
            slots_kernel,
            (jax.ShapeDtypeStruct((slots, out_width), BF), jax.ShapeDtypeStruct((rows, out_width), BF)),
            [SMEM] + [VMEM] * 5,
            [pltpu.VMEM((rows, 3 * width), BF)],
            flops=2 * slots * rows * out_width,
            nbytes=1 << 20,
        )(place, own, near, far, route_col, route_row)
    with jax.named_scope("rows_out"):
        sent = sent.reshape(prompt_count, step_count * CAP, out_width)
        arrived = lax.all_to_all(sent, "prompt", 0, 0, tiled=True).reshape(slots, out_width)
    with jax.named_scope("pages_to_heads"):
        piece = [own[:, c * DH : (c + 1) * DH] for c in range(5)]
        own_kv = jnp.stack(
            [jnp.concatenate([piece[k], piece[v]], axis=1) for k, v in ((2, 1), (3, 2), (4, 3), (0, 4))]
        )
        outgoing = jnp.concatenate([by_head(pages.reshape(-1, pages.shape[2])), own_kv], axis=1)
        groups = [list(range(core, seq_count, 2)) for core in range(2)]
        mine = lax.all_to_all(outgoing, "seq", 0, 0, tiled=True, axis_index_groups=groups)
        other = lax.ppermute(mine, "seq", [(i, i ^ 1) for i in range(seq_count)])
    with jax.named_scope("prefix_part"):
        part = call(
            prefix_kernel,
            jax.ShapeDtypeStruct((slots, out_width + DH), BF),
            [VMEM] * 2,
            flops=4 * slots * head_part * seq_count * DH * DH,
            nbytes=1 << 20,
        )(arrived, prefix)
    with jax.named_scope("rows_back"):
        part = part.reshape(prompt_count, step_count * CAP, out_width + DH)
        back = lax.all_to_all(part, "prompt", 0, 0, tiled=True).reshape(slots, out_width + DH)
    with jax.named_scope("page_part"):
        home, home_stats = call(
            page_kernel,
            (jax.ShapeDtypeStruct((rows, out_width), F32), jax.ShapeDtypeStruct((rows, DH), F32)),
            [SMEM] + [VMEM] * 4,
            flops=4 * rows * head_part * 4096 * DH,
            nbytes=4 << 20,
        )(place, query, parent.reshape(1, rows), mine, other)
    with jax.named_scope("finish"):
        attended = call(
            finish_kernel,
            jax.ShapeDtypeStruct((rows, out_width), BF),
            [VMEM] * 5,
            flops=2 * slots * rows * out_width,
            nbytes=1 << 20,
        )(back, route_col, route_row, home, home_stats)
    return attended.reshape(step_count, row_count, out_width)


def solution(mesh):
    return jax.shard_map(
        body,
        mesh=mesh,
        in_specs=(
            P(None, "prompt", "seq"),
            P(None, "prompt", None),
            P(None, "prompt"),
            P("prompt", "seq", None),
            P("prompt", "seq", None),
        ),
        out_specs=P(None, "prompt", "seq"),
        check_vma=False,
    )
```

```python
import jax
import jax.numpy as jnp
from jax import lax
from jax.experimental import pallas as pl
from jax.experimental.pallas import tpu as pltpu
from jax.sharding import PartitionSpec as P

HQ = 32
KVH = 4
DH = 128
CAP = 2
STAT = 8
PRE = 128
PAGE_ROWS = 512
SCALE = DH ** (-0.5)
BF = jnp.bfloat16
F32 = jnp.float32
NT = (((1,), (1,)), ((), ()))
NN = (((1,), (0,)), ((), ()))
TN = (((0,), (0,)), ((), ()))
VMEM = pl.BlockSpec(memory_space=pltpu.VMEM)
SMEM = pl.BlockSpec(memory_space=pltpu.SMEM)
HBM = pl.BlockSpec(memory_space=pltpu.HBM)


def dot(a, b, dims):
    return lax.dot_general(a, b, dims, preferred_element_type=F32)


def call(kernel, outs, *operands, scratch=(), flops=0, nbytes=0, vmem=24, name=None):
    single = not isinstance(outs, tuple)
    specs = {"v": VMEM, "s": SMEM, "r": HBM}
    result = pl.pallas_call(
        kernel,
        out_shape=(outs,) if single else outs,
        in_specs=[specs[kind] for kind, _ in operands],
        out_specs=(VMEM,) if single else (VMEM,) * len(outs),
        scratch_shapes=list(scratch),
        compiler_params=pltpu.CompilerParams(vmem_limit_bytes=vmem << 20),
        cost_estimate=pl.CostEstimate(flops=flops, bytes_accessed=nbytes, transcendentals=0),
        name=name,
    )(*[array for _, array in operands])
    return result[0] if single else result


def split_kernel(seq_ref, pages_ref, prefix_ref, own_ref, *out_refs):
    chip = seq_ref[0] // 2
    core = lax.rem(seq_ref[0], 2)
    rows = own_ref.shape[0]
    for k, out_ref in enumerate(out_refs):
        target = lax.rem(chip + k, KVH)
        at = 0
        for ref in (pages_ref, prefix_ref):
            count = ref.shape[0]
            for part in range(2):
                cols = pl.ds(pl.multiple_of((part * KVH + target) * DH, DH), DH)
                out_ref[at : at + count, :] = ref[:, cols]
                at += count
        if k == 0:
            out_ref[at : at + rows, :] = own_ref[:, :DH]
            out_ref[at + rows :, :] = own_ref[:, 4 * DH :]
        else:
            chunk = jnp.minimum(2 - core + target, 4)
            out_ref[at:, :] = own_ref[:, pl.ds(pl.multiple_of(chunk * DH, DH), DH)]


def share_kernel(query_ref, *refs):
    out_ref = refs[-1]
    rows = query_ref.shape[0]
    at = 0
    for ref in refs[:-1]:
        out_ref[at : at + 2 * PRE, :] = ref[2 * PAGE_ROWS : 2 * PAGE_ROWS + 2 * PRE, :]
        at += 2 * PRE
    for h in range(query_ref.shape[1] // DH):
        out_ref[at : at + rows, :] = query_ref[:, h * DH : (h + 1) * DH]
        at += rows


def slot_of(route, rank, axis, rows):
    step = lax.broadcasted_iota(jnp.int32, route.shape, axis) >= rows // 2
    return route, step.astype(jnp.int32) * CAP + rank


def ranks(along, across, rows, axis):
    first = lax.broadcasted_iota(jnp.int32, (rows, rows), axis)
    second = lax.broadcasted_iota(jnp.int32, (rows, rows), 1 - axis)
    same = (along == across) & (first < second) & ((first < rows // 2) == (second < rows // 2))
    return jnp.sum(same.astype(jnp.int32), axis=axis, keepdims=True)


def route_both(route_ref):
    row = jnp.concatenate([route_ref[0:1, :], route_ref[1:2, :]], axis=1)
    rows = row.shape[1]
    column = jnp.broadcast_to(row, (rows, rows)).T[:, :1]
    return row, column


def slots_kernel(seq_ref, own_ref, near_ref, far_ref, route_ref, sent_ref, query_ref, line, wide):
    rows = own_ref.shape[0]
    width = own_ref.shape[1]
    heads = query_ref.shape[1] // DH
    count = sent_ref.shape[0] // heads
    line[:, :width] = far_ref[...]
    line[:, width : 2 * width] = near_ref[...]
    line[:, 2 * width :] = own_ref[...]
    first = pl.multiple_of((10 - seq_ref[0]) * DH, DH)
    query = line[:, pl.ds(first, query_ref.shape[1])]
    query_ref[...] = query
    row, column = route_both(route_ref)
    prompt, slot = slot_of(row, ranks(column, row, rows, 0), 1, rows)
    onehot = lax.broadcasted_iota(jnp.int32, (count, rows), 0) == prompt * (2 * CAP) + slot
    onehot = onehot.astype(F32).astype(BF)
    for h in range(heads):
        wide[pl.ds(h, count, stride=heads), :] = dot(onehot, query[:, h * DH : (h + 1) * DH], NN)
    sent_ref[...] = wide[...].astype(BF)


def thirds(value):
    high = value.astype(BF).astype(F32)
    rest = value - high
    middle = rest.astype(BF).astype(F32)
    low = (rest - middle).astype(BF).astype(F32)
    return [high, middle, low]


def prefix_kernel(query_ref, mine_ref, other_ref, out_ref):
    per_message = out_ref.shape[1] - STAT
    wide = 256
    blocks = [(ref, 2 * PRE * k) for ref in (mine_ref, other_ref) for k in range(KVH)]
    values_t = [ref[at + PRE : at + 2 * PRE, :].astype(F32).T.astype(BF) for ref, at in blocks]
    for c in range(query_ref.shape[0] // wide):
        query = query_ref[c * wide : (c + 1) * wide, :]
        tops, totals, parts = [], [], []
        for (ref, at), value_t in zip(blocks, values_t):
            scores = dot(ref[at : at + PRE, :], query, NT) * SCALE
            top = jnp.max(scores, axis=0, keepdims=True)
            weights = jnp.exp(scores - top).astype(BF)
            tops.append(top)
            totals.append(jnp.sum(weights.astype(F32), axis=0, keepdims=True))
            parts.append(dot(value_t, weights, NN))
        top = tops[0]
        for other in tops[1:]:
            top = jnp.maximum(top, other)
        total = jnp.zeros_like(top)
        mixed = jnp.zeros((DH, wide), F32)
        for block_top, block_total, block_part in zip(tops, totals, parts):
            factor = jnp.exp(block_top - top)
            total += block_total * factor
            mixed += block_part * factor
        mixed = (mixed / total).T.astype(BF)
        messages = wide // per_message
        at = c * messages
        out_ref[at : at + messages, :per_message, :] = mixed.reshape(messages, per_message, DH)
        zero = jnp.zeros_like(top)
        stats = jnp.concatenate(thirds(top) + thirds(total) + [zero, zero], axis=0).astype(BF)
        for g in range(wide // DH):
            for i in range(DH // per_message):
                out_ref[at + g * (DH // per_message) + i, per_message:, :] = stats[:, g * DH : (g + 1) * DH]


def page_kernel(seq_ref, mine_ref, other_ref, parent_ref, *refs):
    pieces, kept_ref, sent_ref = refs[:4], refs[4], refs[5]
    first = 2 * PRE * KVH
    half = mine_ref.shape[0] - first
    rows = 2 * parent_ref.shape[1]
    heads = half // rows
    count = PAGE_ROWS
    seg = 16
    tail = 2 * count + 2 * PRE
    query = jnp.concatenate([mine_ref[first:, :], other_ref[first:, :]], axis=0)
    parent = jnp.concatenate([parent_ref[0:1, :], parent_ref[1:2, :]] * (2 * heads), axis=1)
    scores = []
    for ref in pieces:
        every = dot(ref[:count, :], query, NT)
        held = every[:seg, :]
        for j in range(1, count // seg):
            held = jnp.where(parent == j, every[j * seg : (j + 1) * seg, :], held)
        scores.append(held * SCALE)
    top = jnp.max(scores[0], axis=0, keepdims=True)
    for held in scores[1:]:
        top = jnp.maximum(top, jnp.max(held, axis=0, keepdims=True))
    total = jnp.zeros_like(top)
    mixed = jnp.zeros((DH, 2 * half), F32)
    for ref, held in zip(pieces, scores):
        weights = jnp.exp(held - top).astype(BF).astype(F32)
        total += jnp.sum(weights, axis=0, keepdims=True)
        chosen = jnp.concatenate([jnp.where(parent == j, weights, 0.0) for j in range(count // seg)], axis=0)
        mixed += dot(ref[count : 2 * count, :], chosen.astype(BF), TN)
    chip = seq_ref[0] // 2
    own = jnp.where(chip == 0, pieces[1][tail:, :], jnp.where(chip == 1, pieces[2][tail:, :], pieces[3][tail:, :]))
    last = chip == 3
    key = jnp.where(last, pieces[0][tail : tail + rows, :], own).astype(F32).T
    value = jnp.where(last, pieces[0][tail + rows :, :], own).astype(F32).T
    query_t = query.astype(F32).T
    own_score = jnp.concatenate(
        [
            jnp.sum(query_t[:, h * rows : (h + 1) * rows] * key, axis=0, keepdims=True)
            for h in range(2 * heads)
        ],
        axis=1,
    )
    stats = jnp.concatenate([top, total, own_score * SCALE] + [jnp.zeros_like(top)] * 5, axis=0)
    for n, ref in enumerate((kept_ref, sent_ref)):
        ref[:DH, :half] = mixed[:, n * half : (n + 1) * half]
        ref[:DH, half:] = value
        ref[DH:, :half] = stats[:, n * half : (n + 1) * half]
        ref[DH:, half:] = jnp.zeros((STAT, DH), F32)


def merge_kernel(seq_ref, kept_ref, got_ref, out_ref, stat_ref):
    rows = out_ref.shape[0]
    heads = out_ref.shape[1] // DH
    half = heads * rows
    even = lax.rem(seq_ref[0], 2) == 0
    last = seq_ref[0] // 2 == 3
    has_key = even != last
    kept, got = kept_ref[DH:, :half], got_ref[DH:, :half]
    own_score = jnp.where(has_key, kept[2:3, :], got[2:3, :])
    best = jnp.maximum(jnp.maximum(kept[0:1, :], got[0:1, :]), own_score)
    factor_kept = jnp.exp(kept[0:1, :] - best)
    factor_got = jnp.exp(got[0:1, :] - best)
    factor_own = jnp.exp(own_score - best)
    total = kept[1:2, :] * factor_kept + got[1:2, :] * factor_got + factor_own
    value = jnp.where(even, got_ref[:DH, half:], kept_ref[:DH, half:])
    for h in range(heads):
        cols = slice(h * rows, (h + 1) * rows)
        part = kept_ref[:DH, cols] * factor_kept[:, cols] + got_ref[:DH, cols] * factor_got[:, cols]
        part += value * factor_own[:, cols]
        out_ref[:, h * DH : (h + 1) * DH] = part.T
    stats = [line[:, h * rows : (h + 1) * rows] for line in (best, total) for h in range(heads)]
    stats.append(jnp.zeros((DH - 2 * heads, rows), F32))
    stat_ref[...] = jnp.concatenate(stats, axis=0).T


def finish_kernel(prompt_ref, back_ref, route_ref, part_ref, stat_ref, out_ref, wide):
    rows = part_ref.shape[0]
    heads = part_ref.shape[1] // DH
    slots = 2 * CAP
    per_message = slots * heads
    stride = per_message + STAT
    messages = back_ref.shape[0] // stride
    wide[...] = back_ref[...].astype(F32)
    row, column = route_both(route_ref)
    prompt, slot = slot_of(column, ranks(row, column, rows, 1), 0, rows)
    lane = lax.broadcasted_iota(jnp.int32, (rows, slots * messages), 1)
    onehot = (lane == slot * messages + prompt).astype(F32).astype(BF)
    lane = lax.broadcasted_iota(jnp.int32, (rows, messages), 1)
    chosen = (lane == prompt).astype(F32).astype(BF)

    def line(at):
        return wide[pl.ds(at, messages, stride=stride), :].astype(BF)

    found = [dot(chosen, line(per_message + v), NN) for v in range(6)]
    tops = found[0] + found[1] + found[2]
    totals = found[3] + found[4] + found[5]
    group = lax.rem(prompt_ref[0], DH // per_message)
    lane = lax.broadcasted_iota(jnp.int32, (rows, DH), 1)
    stats = stat_ref[...]
    for h in range(heads):
        cols = slice(h * DH, (h + 1) * DH)
        lines = jnp.concatenate([line(s * heads + h) for s in range(slots)], axis=0)
        got = dot(onehot, lines, NN)
        mask = lane == group * per_message + slot * heads + h
        prefix_top = jnp.sum(jnp.where(mask, tops, 0.0), axis=1, keepdims=True)
        prefix_total = jnp.sum(jnp.where(mask, totals, 0.0), axis=1, keepdims=True)
        home_top = stats[:, h : h + 1]
        home_total = stats[:, heads + h : heads + h + 1]
        best = jnp.maximum(prefix_top, home_top)
        factor_prefix = jnp.exp(prefix_top - best) * prefix_total
        factor_home = jnp.exp(home_top - best)
        denom = factor_prefix + home_total * factor_home
        numer = got * factor_prefix + part_ref[:, cols] * factor_home
        out_ref[:, cols] = (numer / denom).astype(BF)


def body(beam_rows, route, parent, prefix_kv, pages):
    prompt_count = lax.axis_size("prompt")
    seq_count = lax.axis_size("seq")
    step_count, row_count, width = beam_rows.shape
    rows = step_count * row_count
    head_part = HQ // seq_count
    out_width = head_part * DH
    per_message = step_count * CAP * head_part
    slots = prompt_count * per_message
    seq_at = lax.axis_index("seq").astype(jnp.int32).reshape(1)
    prompt_at = lax.axis_index("prompt").astype(jnp.int32).reshape(1)
    own = beam_rows.reshape(rows, width)
    route = route.reshape(step_count, row_count)
    swap = [(i, i ^ 1) for i in range(seq_count)]

    def turn(value, k):
        return lax.ppermute(value, "seq", [(i, (i + 2 * k) % seq_count) for i in range(seq_count)])

    with jax.named_scope("rows_to_heads"):
        near = lax.ppermute(own, "seq", [(i, i + 1) for i in range(seq_count - 1)])
        far = lax.ppermute(own, "seq", [(4, 6), (5, 7)])
    with jax.named_scope("tokens_to_heads"):
        count = pages.shape[0] * pages.shape[1]
        pre = prefix_kv.shape[1]
        split = call(
            split_kernel,
            tuple(
                jax.ShapeDtypeStruct((2 * count + 2 * pre + (2 if k == 0 else 1) * rows, DH), BF) for k in range(4)
            ),
            ("s", seq_at), ("v", pages.reshape(count, pages.shape[2])), ("v", prefix_kv[0]), ("v", own),
            nbytes=3 << 20,
        )
        *split, near, far = lax.optimization_barrier((*split, near, far))
        pieces = [split[0]] + [turn(split[k], k) for k in range(1, 4)]
    with jax.named_scope("slots"):
        sent, query = call(
            slots_kernel,
            (jax.ShapeDtypeStruct((slots, DH), BF), jax.ShapeDtypeStruct((rows, out_width), BF)),
            ("s", seq_at), ("v", own), ("v", near), ("v", far), ("v", route),
            scratch=[pltpu.VMEM((rows, 3 * width), BF), pltpu.VMEM((slots, DH), F32)],
            flops=2 * slots * rows * DH,
            nbytes=1 << 20,
        )
    with jax.named_scope("rows_out"):
        sent = sent.reshape(prompt_count, per_message, DH)
        arrived = lax.all_to_all(sent, "prompt", 0, 0, tiled=True).reshape(slots, DH)
    with jax.named_scope("share_cores"):
        shared = call(
            share_kernel,
            jax.ShapeDtypeStruct((KVH * 2 * pre + rows * head_part, DH), BF),
            ("v", query), *[("v", piece) for piece in pieces],
            nbytes=1 << 20,
        )
        other = lax.ppermute(shared, "seq", swap)
    with jax.named_scope("prefix_part"):
        part = call(
            prefix_kernel,
            jax.ShapeDtypeStruct((prompt_count, per_message + STAT, DH), BF),
            ("v", arrived), ("v", shared), ("v", other),
            flops=4 * slots * 1024 * DH,
            nbytes=1 << 20,
        )
    with jax.named_scope("rows_back"):
        back = lax.all_to_all(part, "prompt", 0, 0, tiled=True).reshape(-1, DH)
    with jax.named_scope("page_part"):
        payload = jax.ShapeDtypeStruct((DH + STAT, rows * head_part + DH), F32)
        kept, lent = call(
            page_kernel,
            (payload, payload),
            ("s", seq_at), ("v", shared), ("v", other), ("v", parent), *[("v", piece) for piece in pieces],
            flops=4 * rows * head_part * 4096 * DH,
            nbytes=2 << 20,
        )
        got = lax.ppermute(lent, "seq", swap)
    with jax.named_scope("page_merge"):
        home = call(
            merge_kernel,
            (jax.ShapeDtypeStruct((rows, out_width), F32), jax.ShapeDtypeStruct((rows, DH), F32)),
            ("s", seq_at), ("v", kept), ("v", got),
            flops=1 << 20,
            nbytes=1 << 20,
        )
    with jax.named_scope("finish"):
        attended = call(
            finish_kernel,
            jax.ShapeDtypeStruct((rows, out_width), BF),
            ("s", prompt_at), ("v", back), ("v", route), *[("v", value) for value in home],
            scratch=[pltpu.VMEM((prompt_count * (per_message + STAT), DH), F32)],
            flops=2 * slots * rows * DH,
            nbytes=1 << 20,
        )
    return attended.reshape(step_count, row_count, out_width)


def solution(mesh):
    return jax.shard_map(
        body,
        mesh=mesh,
        in_specs=(
            P(None, "prompt", "seq"),
            P(None, "prompt", None),
            P(None, "prompt"),
            P("prompt", "seq", None),
            P("prompt", "seq", None),
        ),
        out_specs=P(None, "prompt", "seq"),
        check_vma=False,
    )
```

```python
import jax
import jax.numpy as jnp
from jax import lax
from jax.experimental import pallas as pl
from jax.experimental.pallas import tpu as pltpu
from jax.sharding import PartitionSpec as P

HQ = 32
KVH = 4
DH = 128
CAP = 2
STAT = 2
ROWSTAT = 8
MESSAGE = 16 + STAT
PRE = 128
PAGE_ROWS = 512
SCALE = DH ** (-0.5)
LOG2E = 1.4426950408889634
BF = jnp.bfloat16
F32 = jnp.float32
NT = (((1,), (1,)), ((), ()))
NN = (((1,), (0,)), ((), ()))
TN = (((0,), (0,)), ((), ()))
VMEM = pl.BlockSpec(memory_space=pltpu.VMEM)
SMEM = pl.BlockSpec(memory_space=pltpu.SMEM)
HBM = pl.BlockSpec(memory_space=pltpu.HBM)


def dot(a, b, dims):
    return lax.dot_general(a, b, dims, preferred_element_type=F32)


def call(kernel, outs, *operands, scratch=(), flops=0, nbytes=0, vmem=24, out="v", name=None):
    single = not isinstance(outs, tuple)
    specs = {"v": VMEM, "s": SMEM, "r": HBM}
    result = pl.pallas_call(
        kernel,
        out_shape=(outs,) if single else outs,
        in_specs=[specs[kind] for kind, _ in operands],
        out_specs=(specs[out],) * (1 if single else len(outs)),
        scratch_shapes=list(scratch),
        compiler_params=pltpu.CompilerParams(vmem_limit_bytes=vmem << 20),
        cost_estimate=pl.CostEstimate(flops=flops, bytes_accessed=nbytes, transcendentals=0),
        name=name,
    )(*[array for _, array in operands])
    return result[0] if single else result


def split_kernel(seq_ref, pages_ref, prefix_ref, own_ref, *refs):
    count = len(refs) // 2
    out_refs, held, sems = refs[:count], refs[count:-1], refs[-1]
    chip = seq_ref[0] // 2
    core = lax.rem(seq_ref[0], 2)
    order = (1, 3, 2, 0)
    fetched = {}
    used = count
    for k in order:
        target = lax.rem(chip + k, KVH)
        pieces = [
            (ref, pl.ds(pl.multiple_of((part * KVH + target) * DH, DH), DH))
            for ref in (pages_ref, prefix_ref)
            for part in range(2)
        ]
        if k == 0:
            pieces += [(own_ref, pl.ds(0, DH)), (own_ref, pl.ds(4 * DH, DH))]
        else:
            chunk = jnp.minimum(2 - core + target, 4)
            pieces.append((own_ref, pl.ds(pl.multiple_of(chunk * DH, DH), DH)))
        at, fetched[k] = 0, []
        for source, cols in pieces:
            size = source.shape[0]
            fetched[k].append(
                pltpu.make_async_copy(source.at[:, cols], held[k].at[at : at + size, :], sems.at[used])
            )
            at += size
            used += 1
    for k in order:
        for copy in fetched[k]:
            copy.start()
    written = [pltpu.make_async_copy(held[k], out_refs[k], sems.at[k]) for k in range(count)]
    for k in order:
        for copy in fetched[k]:
            copy.wait()
        written[k].start()
    for copy in written:
        copy.wait()


def share_kernel(query_ref, *refs):
    out_ref = refs[-1]
    rows = query_ref.shape[0]
    at = 0
    for ref in refs[:-1]:
        out_ref[at : at + 2 * PRE, :] = ref[2 * PAGE_ROWS : 2 * PAGE_ROWS + 2 * PRE, :]
        at += 2 * PRE
    for h in range(query_ref.shape[1] // DH):
        out_ref[at : at + rows, :] = query_ref[:, h * DH : (h + 1) * DH]
        at += rows


def slot_of(route, rank, axis, rows):
    step = lax.broadcasted_iota(jnp.int32, route.shape, axis) >= rows // 2
    return route, step.astype(jnp.int32) * CAP + rank


def ranks(along, across, rows, axis):
    first = lax.broadcasted_iota(jnp.int32, (rows, rows), axis)
    second = lax.broadcasted_iota(jnp.int32, (rows, rows), 1 - axis)
    same = (along == across) & (first < second) & ((first < rows // 2) == (second < rows // 2))
    return jnp.sum(same.astype(jnp.int32), axis=axis, keepdims=True)


def route_both(route_ref):
    row = jnp.concatenate([route_ref[0:1, :], route_ref[1:2, :]], axis=1)
    rows = row.shape[1]
    column = jnp.broadcast_to(row, (rows, rows)).T[:, :1]
    return row, column


def slots_kernel(seq_ref, own_ref, near_ref, far_ref, route_ref, sent_ref, query_ref, line, wide):
    rows = own_ref.shape[0]
    width = own_ref.shape[1]
    heads = query_ref.shape[1] // DH
    count = sent_ref.shape[0] // heads
    line[:, 3 * DH : width] = far_ref[...]
    line[:, width : 2 * width] = near_ref[...]
    line[:, 2 * width :] = own_ref[...]
    first = pl.multiple_of((10 - seq_ref[0]) * DH, DH)
    query = line[:, pl.ds(first, query_ref.shape[1])]
    query_ref[...] = query
    row, column = route_both(route_ref)
    prompt, slot = slot_of(row, ranks(column, row, rows, 0), 1, rows)
    onehot = lax.broadcasted_iota(jnp.int32, (count, rows), 0) == prompt * (2 * CAP) + slot
    onehot = onehot.astype(F32).astype(BF)
    for h in range(heads):
        wide[pl.ds(h, count, stride=heads), :] = dot(onehot, query[:, h * DH : (h + 1) * DH], NN)
    sent_ref[...] = wide[...].astype(BF)


def thirds(value):
    high = value.astype(BF).astype(F32)
    rest = value - high
    middle = rest.astype(BF).astype(F32)
    low = (rest - middle).astype(BF).astype(F32)
    return [high, middle, low]


def prefix_kernel(query_ref, mine_ref, other_ref, out_ref, held):
    messages = out_ref.shape[0] // MESSAGE
    per_message = MESSAGE - STAT
    stats = []
    wide = 256
    blocks = [(ref, 2 * PRE * k) for ref in (mine_ref, other_ref) for k in range(KVH)]
    values_t = [ref[at + PRE : at + 2 * PRE, :].astype(F32).T.astype(BF) for ref, at in blocks]
    for c in range(query_ref.shape[0] // wide):
        query = query_ref[c * wide : (c + 1) * wide, :]
        tops, totals, parts = [], [], []
        for (ref, at), value_t in zip(blocks, values_t):
            scores = dot(ref[at : at + PRE, :], query, NT)
            top = jnp.max(scores, axis=0, keepdims=True)
            weights = jnp.exp2((scores - top) * (SCALE * LOG2E)).astype(BF)
            tops.append(top)
            totals.append(jnp.sum(weights.astype(F32), axis=0, keepdims=True))
            parts.append(dot(value_t, weights, NN))
        top = tops[0]
        for other in tops[1:]:
            top = jnp.maximum(top, other)
        total = jnp.zeros_like(top)
        mixed = jnp.zeros((DH, wide), F32)
        for block_top, block_total, block_part in zip(tops, totals, parts):
            factor = jnp.exp2((block_top - top) * (SCALE * LOG2E))
            total += block_total * factor
            mixed += block_part * factor
        top = top * SCALE
        mixed = (mixed * (1.0 / total)).T
        for i in range(wide // per_message):
            at = (c * wide // per_message + i) * MESSAGE
            held[at : at + per_message, :] = mixed[i * per_message : (i + 1) * per_message, :]
        stats += [jnp.concatenate(thirds(top) + thirds(total), axis=0)]
    stats = jnp.concatenate(stats, axis=1)
    terms = stats.shape[0]
    near_by = DH // per_message
    line = lax.broadcasted_iota(jnp.int32, (near_by, DH), 0)
    lane = lax.broadcasted_iota(jnp.int32, (near_by, DH), 1)
    mine = lane // per_message == line
    spread = jnp.concatenate(
        [
            jnp.concatenate(
                [jnp.where(mine, stats[v : v + 1, g * DH : (g + 1) * DH], 0.0) for v in range(terms)], axis=1
            )
            for g in range(messages // near_by)
        ],
        axis=0,
    ).astype(BF)
    source = lax.broadcasted_iota(jnp.int32, (terms * DH, DH), 0)
    target = lax.broadcasted_iota(jnp.int32, (terms * DH, DH), 1)
    place = (source // DH) * per_message + source % per_message
    held_stats = dot(spread, (place == target).astype(F32).astype(BF), NN)
    held[pl.ds(per_message, messages, stride=MESSAGE), :] = held_stats
    held[pl.ds(per_message + 1, messages, stride=MESSAGE), :] = jnp.zeros((messages, DH), F32)
    out_ref[...] = held[...].astype(BF)


def page_kernel(seq_ref, mine_ref, other_ref, parent_ref, *refs):
    pieces, kept_ref, sent_ref = refs[:4], refs[4], refs[5]
    first = 2 * PRE * KVH
    half = mine_ref.shape[0] - first
    rows = 2 * parent_ref.shape[1]
    heads = half // rows
    count = PAGE_ROWS
    seg = 16
    tail = 2 * count + 2 * PRE
    query = jnp.concatenate([mine_ref[first:, :], other_ref[first:, :]], axis=0)
    parent = jnp.concatenate([parent_ref[0:1, :], parent_ref[1:2, :]] * (2 * heads), axis=1)
    scores = []
    for ref in pieces:
        every = dot(ref[:count, :], query, NT)
        held = every[:seg, :]
        for j in range(1, count // seg):
            held = jnp.where(parent == j, every[j * seg : (j + 1) * seg, :], held)
        scores.append(held * SCALE)
    top = jnp.max(scores[0], axis=0, keepdims=True)
    for held in scores[1:]:
        top = jnp.maximum(top, jnp.max(held, axis=0, keepdims=True))
    total = jnp.zeros_like(top)
    mixed = jnp.zeros((DH, 2 * half), F32)
    for ref, held in zip(pieces, scores):
        weights = jnp.exp(held - top).astype(BF).astype(F32)
        total += jnp.sum(weights, axis=0, keepdims=True)
        chosen = jnp.concatenate([jnp.where(parent == j, weights, 0.0) for j in range(count // seg)], axis=0)
        mixed += dot(ref[count : 2 * count, :], chosen.astype(BF), TN)
    chip = seq_ref[0] // 2
    own = jnp.where(chip == 0, pieces[1][tail:, :], jnp.where(chip == 1, pieces[2][tail:, :], pieces[3][tail:, :]))
    last = chip == 3
    key = jnp.where(last, pieces[0][tail : tail + rows, :], own).astype(F32).T
    value = jnp.where(last, pieces[0][tail + rows :, :], own).astype(F32).T
    query_t = query.astype(F32).T
    own_score = jnp.concatenate(
        [
            jnp.sum(query_t[:, h * rows : (h + 1) * rows] * key, axis=0, keepdims=True)
            for h in range(2 * heads)
        ],
        axis=1,
    )
    stats = jnp.concatenate([top, total, own_score * SCALE] + [jnp.zeros_like(top)] * 5, axis=0)
    for n, ref in enumerate((kept_ref, sent_ref)):
        ref[:DH, :half] = mixed[:, n * half : (n + 1) * half]
        ref[:DH, half:] = value
        ref[DH:, :half] = stats[:, n * half : (n + 1) * half]
        ref[DH:, half:] = jnp.zeros((ROWSTAT, DH), F32)


def merge_kernel(seq_ref, kept_ref, got_ref, route_ref, out_ref, stat_ref, pick_ref, mask_ref):
    rows = out_ref.shape[0]
    heads = out_ref.shape[1] // DH
    half = heads * rows
    even = lax.rem(seq_ref[0], 2) == 0
    last = seq_ref[0] // 2 == 3
    has_key = even != last
    kept, got = kept_ref[DH:, :half], got_ref[DH:, :half]
    own_score = jnp.where(has_key, kept[2:3, :], got[2:3, :])
    best = jnp.maximum(jnp.maximum(kept[0:1, :], got[0:1, :]), own_score)
    factor_kept = jnp.exp(kept[0:1, :] - best)
    factor_got = jnp.exp(got[0:1, :] - best)
    factor_own = jnp.exp(own_score - best)
    total = kept[1:2, :] * factor_kept + got[1:2, :] * factor_got + factor_own
    value = jnp.where(even, got_ref[:DH, half:], kept_ref[:DH, half:])
    for h in range(heads):
        cols = slice(h * rows, (h + 1) * rows)
        part = kept_ref[:DH, cols] * factor_kept[:, cols] + got_ref[:DH, cols] * factor_got[:, cols]
        part += value * factor_own[:, cols]
        out_ref[:, h * DH : (h + 1) * DH] = part.T
    stats = [line[:, h * rows : (h + 1) * rows] for line in (best, total) for h in range(heads)]
    stats.append(jnp.zeros((DH - 2 * heads, rows), F32))
    stat_ref[...] = jnp.concatenate(stats, axis=0).T
    slots = 2 * CAP
    messages = pick_ref.shape[1] // (slots + 1)
    row, column = route_both(route_ref)
    prompt, slot = slot_of(column, ranks(row, column, rows, 1), 0, rows)
    lane = lax.broadcasted_iota(jnp.int32, (rows, slots * messages), 1)
    pick_ref[:, : slots * messages] = (lane == slot * messages + prompt).astype(F32).astype(BF)
    lane = lax.broadcasted_iota(jnp.int32, (rows, messages), 1)
    pick_ref[:, slots * messages :] = (lane == prompt).astype(F32).astype(BF)
    lane = lax.broadcasted_iota(jnp.int32, (rows, DH), 1)
    for h in range(heads):
        mask_ref[:, h * DH : (h + 1) * DH] = (lane % (slots * heads) == slot * heads + h).astype(F32)


def finish_kernel(back_ref, part_ref, stat_ref, pick_ref, mask_ref, out_ref, wide):
    heads = part_ref.shape[1] // DH
    slots = 2 * CAP
    per_message = slots * heads
    stride = MESSAGE
    messages = back_ref.shape[0] // stride
    wide[...] = back_ref[...].astype(F32)
    onehot = pick_ref[:, : slots * messages]
    chosen = pick_ref[:, slots * messages :]

    def line(at):
        return wide[pl.ds(at, messages, stride=stride), :].astype(BF)

    found = dot(chosen, line(per_message), NN)
    lane = lax.broadcasted_iota(jnp.int32, found.shape, 1)
    tops = jnp.where(lane < 3 * per_message, found, 0.0)
    totals = found - tops
    stats = stat_ref[...]
    for h in range(heads):
        cols = slice(h * DH, (h + 1) * DH)
        lines = jnp.concatenate([line(s * heads + h) for s in range(slots)], axis=0)
        got = dot(onehot, lines, NN)
        mask = mask_ref[:, cols]
        prefix_top = jnp.sum(tops * mask, axis=1, keepdims=True)
        prefix_total = jnp.sum(totals * mask, axis=1, keepdims=True)
        home_top = stats[:, h : h + 1]
        home_total = stats[:, heads + h : heads + h + 1]
        best = jnp.maximum(prefix_top, home_top)
        factor_prefix = jnp.exp(prefix_top - best) * prefix_total
        factor_home = jnp.exp(home_top - best)
        scale = 1.0 / (factor_prefix + home_total * factor_home)
        mixed = got * (factor_prefix * scale) + part_ref[:, cols] * (factor_home * scale)
        out_ref[:, cols] = mixed.astype(BF)


def body(beam_rows, route, parent, prefix_kv, pages):
    prompt_count = lax.axis_size("prompt")
    seq_count = lax.axis_size("seq")
    step_count, row_count, width = beam_rows.shape
    rows = step_count * row_count
    head_part = HQ // seq_count
    out_width = head_part * DH
    per_message = step_count * CAP * head_part
    slots = prompt_count * per_message
    seq_at = lax.axis_index("seq").astype(jnp.int32).reshape(1)
    own = beam_rows.reshape(rows, width)
    route = route.reshape(step_count, row_count)
    swap = [(i, i ^ 1) for i in range(seq_count)]

    def turn(value, k):
        return lax.ppermute(value, "seq", [(i, (i + 2 * k) % seq_count) for i in range(seq_count)])

    with jax.named_scope("rows_to_heads"):
        near = lax.ppermute(own, "seq", [(i, i + 1) for i in range(seq_count - 1)])
        far = lax.ppermute(own[:, 3 * DH :], "seq", [(4, 6), (5, 7)])
    with jax.named_scope("tokens_to_heads"):
        count = pages.shape[0] * pages.shape[1]
        pre = prefix_kv.shape[1]
        split = call(
            split_kernel,
            tuple(
                jax.ShapeDtypeStruct((2 * count + 2 * pre + (2 if k == 0 else 1) * rows, DH), BF) for k in range(4)
            ),
            ("s", seq_at), ("r", pages.reshape(count, pages.shape[2])), ("r", prefix_kv[0]), ("r", own),
            scratch=[
                pltpu.VMEM((2 * count + 2 * pre + (2 if k == 0 else 1) * rows, DH), BF) for k in range(4)
            ] + [pltpu.SemaphoreType.DMA((25,))],
            nbytes=3 << 20,
            vmem=58,
            out="r",
        )
        *split, near, far = lax.optimization_barrier((*split, near, far))
        pieces = [split[0]] + [turn(split[k], k) for k in range(1, 4)]
    with jax.named_scope("slots"):
        sent, query = call(
            slots_kernel,
            (jax.ShapeDtypeStruct((slots, DH), BF), jax.ShapeDtypeStruct((rows, out_width), BF)),
            ("s", seq_at), ("v", own), ("v", near), ("v", far), ("v", route),
            scratch=[pltpu.VMEM((rows, 3 * width), BF), pltpu.VMEM((slots, DH), F32)],
            flops=2 * slots * rows * DH,
            nbytes=1 << 20,
        )
    with jax.named_scope("rows_out"):
        sent = sent.reshape(prompt_count, per_message, DH)
        arrived = lax.all_to_all(sent, "prompt", 0, 0, tiled=True).reshape(slots, DH)
    with jax.named_scope("share_cores"):
        shared = call(
            share_kernel,
            jax.ShapeDtypeStruct((KVH * 2 * pre + rows * head_part, DH), BF),
            ("v", query), *[("v", piece) for piece in pieces],
            nbytes=1 << 20,
        )
        other = lax.ppermute(shared, "seq", swap)
    with jax.named_scope("prefix_part"):
        part = call(
            prefix_kernel,
            jax.ShapeDtypeStruct((prompt_count * MESSAGE, DH), BF),
            ("v", arrived), ("v", shared), ("v", other),
            scratch=[pltpu.VMEM((prompt_count * MESSAGE, DH), F32)],
            flops=4 * slots * 1024 * DH,
            nbytes=1 << 20,
        )
    with jax.named_scope("rows_back"):
        part = part.reshape(prompt_count, MESSAGE // 2, 2, DH)
        back = lax.all_to_all(part, "prompt", 0, 0, tiled=True).reshape(-1, DH)
    with jax.named_scope("page_part"):
        payload = jax.ShapeDtypeStruct((DH + ROWSTAT, rows * head_part + DH), F32)
        kept, lent = call(
            page_kernel,
            (payload, payload),
            ("s", seq_at), ("v", shared), ("v", other), ("v", parent), *[("v", piece) for piece in pieces],
            flops=4 * rows * head_part * 4096 * DH,
            nbytes=2 << 20,
        )
        got = lax.ppermute(lent, "seq", swap)
    with jax.named_scope("page_merge"):
        merged = call(
            merge_kernel,
            (
                jax.ShapeDtypeStruct((rows, out_width), F32),
                jax.ShapeDtypeStruct((rows, DH), F32),
                jax.ShapeDtypeStruct((rows, (step_count * CAP + 1) * prompt_count), BF),
                jax.ShapeDtypeStruct((rows, out_width), F32),
            ),
            ("s", seq_at), ("v", kept), ("v", got), ("v", route),
            flops=1 << 20,
            nbytes=1 << 20,
        )
    with jax.named_scope("finish"):
        attended = call(
            finish_kernel,
            jax.ShapeDtypeStruct((rows, out_width), BF),
            ("v", back), *[("v", value) for value in merged],
            scratch=[pltpu.VMEM((prompt_count * MESSAGE, DH), F32)],
            flops=2 * slots * rows * DH,
            nbytes=1 << 20,
        )
    return attended.reshape(step_count, row_count, out_width)


def solution(mesh):
    return jax.shard_map(
        body,
        mesh=mesh,
        in_specs=(
            P(None, "prompt", "seq"),
            P(None, "prompt", None),
            P(None, "prompt"),
            P("prompt", "seq", None),
            P("prompt", "seq", None),
        ),
        out_specs=P(None, "prompt", "seq"),
        check_vma=False,
    )
```

```python
import jax
import jax.numpy as jnp
from jax import lax
from jax.experimental import pallas as pl
from jax.experimental.pallas import tpu as pltpu
from jax.sharding import PartitionSpec as P

HQ = 32
KVH = 4
DH = 128
CAP = 2
STAT = 2
ROWSTAT = 8
MESSAGE = 16 + STAT
PRE = 128
PAGE_ROWS = 512
SCALE = DH ** (-0.5)
LOG2E = 1.4426950408889634
BF = jnp.bfloat16
F32 = jnp.float32
NT = (((1,), (1,)), ((), ()))
NN = (((1,), (0,)), ((), ()))
TN = (((0,), (0,)), ((), ()))
VMEM = pl.BlockSpec(memory_space=pltpu.VMEM)
SMEM = pl.BlockSpec(memory_space=pltpu.SMEM)
HBM = pl.BlockSpec(memory_space=pltpu.HBM)


def dot(a, b, dims):
    return lax.dot_general(a, b, dims, preferred_element_type=F32)


def call(kernel, outs, *operands, scratch=(), flops=0, nbytes=0, vmem=24, out="v", name=None):
    single = not isinstance(outs, tuple)
    specs = {"v": VMEM, "s": SMEM, "r": HBM}
    result = pl.pallas_call(
        kernel,
        out_shape=(outs,) if single else outs,
        in_specs=[specs[kind] for kind, _ in operands],
        out_specs=(specs[out],) * (1 if single else len(outs)),
        scratch_shapes=list(scratch),
        compiler_params=pltpu.CompilerParams(vmem_limit_bytes=vmem << 20),
        cost_estimate=pl.CostEstimate(flops=flops, bytes_accessed=nbytes, transcendentals=0),
        name=name,
    )(*[array for _, array in operands])
    return result[0] if single else result


def split_kernel(seq_ref, pages_ref, prefix_ref, own_ref, *refs):
    count = len(refs) // 2
    out_refs, held, sems = refs[:count], refs[count:-1], refs[-1]
    chip = seq_ref[0] // 2
    core = lax.rem(seq_ref[0], 2)
    order = (1, 3, 2, 0)
    fetched = {}
    used = count
    for k in order:
        target = lax.rem(chip + k, KVH)
        pieces = [
            (ref, pl.ds(pl.multiple_of((part * KVH + target) * DH, DH), DH))
            for ref in (pages_ref, prefix_ref)
            for part in range(2)
        ]
        if k == 0:
            pieces += [(own_ref, pl.ds(0, DH)), (own_ref, pl.ds(4 * DH, DH))]
        else:
            chunk = jnp.minimum(2 - core + target, 4)
            pieces.append((own_ref, pl.ds(pl.multiple_of(chunk * DH, DH), DH)))
        at, fetched[k] = 0, []
        for source, cols in pieces:
            size = source.shape[0]
            fetched[k].append(
                pltpu.make_async_copy(source.at[:, cols], held[k].at[at : at + size, :], sems.at[used])
            )
            at += size
            used += 1
    for k in order:
        for copy in fetched[k]:
            copy.start()
    written = [pltpu.make_async_copy(held[k], out_refs[k], sems.at[k]) for k in range(count)]
    for k in order:
        for copy in fetched[k]:
            copy.wait()
        written[k].start()
    for copy in written:
        copy.wait()


def share_kernel(query_ref, *refs):
    out_ref = refs[-1]
    rows = query_ref.shape[0]
    at = 0
    for ref in refs[:-1]:
        out_ref[at : at + 2 * PRE, :] = ref[2 * PAGE_ROWS : 2 * PAGE_ROWS + 2 * PRE, :]
        at += 2 * PRE
    for h in range(query_ref.shape[1] // DH):
        out_ref[at : at + rows, :] = query_ref[:, h * DH : (h + 1) * DH]
        at += rows


def slot_of(route, rank, axis, rows):
    step = lax.broadcasted_iota(jnp.int32, route.shape, axis) >= rows // 2
    return route, step.astype(jnp.int32) * CAP + rank


def ranks(along, across, rows, axis):
    first = lax.broadcasted_iota(jnp.int32, (rows, rows), axis)
    second = lax.broadcasted_iota(jnp.int32, (rows, rows), 1 - axis)
    same = (along == across) & (first < second) & ((first < rows // 2) == (second < rows // 2))
    return jnp.sum(same.astype(jnp.int32), axis=axis, keepdims=True)


def route_both(route_ref):
    row = jnp.concatenate([route_ref[0:1, :], route_ref[1:2, :]], axis=1)
    rows = row.shape[1]
    column = jnp.broadcast_to(row, (rows, rows)).T[:, :1]
    return row, column


def slots_kernel(seq_ref, own_ref, near_ref, far_ref, route_ref, sent_ref, query_ref, line, wide):
    rows = own_ref.shape[0]
    width = own_ref.shape[1]
    heads = query_ref.shape[1] // DH
    count = sent_ref.shape[0] // heads
    line[:, 3 * DH : width] = far_ref[...]
    line[:, width : 2 * width] = near_ref[...]
    line[:, 2 * width :] = own_ref[...]
    first = pl.multiple_of((10 - seq_ref[0]) * DH, DH)
    query = line[:, pl.ds(first, query_ref.shape[1])]
    query_ref[...] = query
    row, column = route_both(route_ref)
    prompt, slot = slot_of(row, ranks(column, row, rows, 0), 1, rows)
    onehot = lax.broadcasted_iota(jnp.int32, (count, rows), 0) == prompt * (2 * CAP) + slot
    onehot = onehot.astype(F32).astype(BF)
    for h in range(heads):
        wide[pl.ds(h, count, stride=heads), :] = dot(onehot, query[:, h * DH : (h + 1) * DH], NN)
    sent_ref[...] = wide[...].astype(BF)


def thirds(value):
    high = value.astype(BF).astype(F32)
    rest = value - high
    middle = rest.astype(BF).astype(F32)
    low = (rest - middle).astype(BF).astype(F32)
    return [high, middle, low]


def prefix_kernel(query_ref, mine_ref, other_ref, out_ref, held):
    messages = out_ref.shape[0] // MESSAGE
    per_message = MESSAGE - STAT
    stats = []
    wide = 256
    blocks = [(ref, 2 * PRE * k) for ref in (mine_ref, other_ref) for k in range(KVH)]
    values_t = [ref[at + PRE : at + 2 * PRE, :].astype(F32).T.astype(BF) for ref, at in blocks]
    for c in range(query_ref.shape[0] // wide):
        query = query_ref[c * wide : (c + 1) * wide, :]
        tops, totals, parts = [], [], []
        for (ref, at), value_t in zip(blocks, values_t):
            scores = dot(ref[at : at + PRE, :], query, NT)
            top = jnp.max(scores, axis=0, keepdims=True)
            weights = jnp.exp2((scores - top) * (SCALE * LOG2E)).astype(BF)
            tops.append(top)
            totals.append(jnp.sum(weights.astype(F32), axis=0, keepdims=True))
            parts.append(dot(value_t, weights, NN))
        top = tops[0]
        for other in tops[1:]:
            top = jnp.maximum(top, other)
        total = jnp.zeros_like(top)
        mixed = jnp.zeros((DH, wide), F32)
        for block_top, block_total, block_part in zip(tops, totals, parts):
            factor = jnp.exp2((block_top - top) * (SCALE * LOG2E))
            total += block_total * factor
            mixed += block_part * factor
        top = top * SCALE
        mixed = (mixed * (1.0 / total)).T
        for i in range(wide // per_message):
            at = (c * wide // per_message + i) * MESSAGE
            held[at : at + per_message, :] = mixed[i * per_message : (i + 1) * per_message, :]
        stats += [jnp.concatenate(thirds(top) + thirds(total), axis=0)]
    stats = jnp.concatenate(stats, axis=1)
    terms = stats.shape[0]
    near_by = DH // per_message
    line = lax.broadcasted_iota(jnp.int32, (near_by, DH), 0)
    lane = lax.broadcasted_iota(jnp.int32, (near_by, DH), 1)
    mine = lane // per_message == line
    spread = jnp.concatenate(
        [
            jnp.concatenate(
                [jnp.where(mine, stats[v : v + 1, g * DH : (g + 1) * DH], 0.0) for v in range(terms)], axis=1
            )
            for g in range(messages // near_by)
        ],
        axis=0,
    ).astype(BF)
    source = lax.broadcasted_iota(jnp.int32, (terms * DH, DH), 0)
    target = lax.broadcasted_iota(jnp.int32, (terms * DH, DH), 1)
    place = (source // DH) * per_message + source % per_message
    held_stats = dot(spread, (place == target).astype(F32).astype(BF), NN)
    held[pl.ds(per_message, messages, stride=MESSAGE), :] = held_stats
    held[pl.ds(per_message + 1, messages, stride=MESSAGE), :] = jnp.zeros((messages, DH), F32)
    out_ref[...] = held[...].astype(BF)


def page_kernel(seq_ref, mine_ref, other_ref, parent_ref, *refs):
    pieces, kept_ref, sent_ref = refs[:4], refs[4], refs[5]
    first = 2 * PRE * KVH
    half = mine_ref.shape[0] - first
    rows = 2 * parent_ref.shape[1]
    heads = half // rows
    count = PAGE_ROWS
    seg = 16
    tail = 2 * count + 2 * PRE
    query = jnp.concatenate([mine_ref[first:, :], other_ref[first:, :]], axis=0)
    parent = jnp.concatenate([parent_ref[0:1, :], parent_ref[1:2, :]] * (2 * heads), axis=1)
    scores = []
    for ref in pieces:
        every = dot(ref[:count, :], query, NT)
        held = every[:seg, :]
        for j in range(1, count // seg):
            held = jnp.where(parent == j, every[j * seg : (j + 1) * seg, :], held)
        scores.append(held * SCALE)
    top = jnp.max(scores[0], axis=0, keepdims=True)
    for held in scores[1:]:
        top = jnp.maximum(top, jnp.max(held, axis=0, keepdims=True))
    total = jnp.zeros_like(top)
    mixed = jnp.zeros((DH, 2 * half), F32)
    for ref, held in zip(pieces, scores):
        weights = jnp.exp(held - top).astype(BF).astype(F32)
        total += jnp.sum(weights, axis=0, keepdims=True)
        chosen = jnp.concatenate([jnp.where(parent == j, weights, 0.0) for j in range(count // seg)], axis=0)
        mixed += dot(ref[count : 2 * count, :], chosen.astype(BF), TN)
    chip = seq_ref[0] // 2
    own = jnp.where(chip == 0, pieces[1][tail:, :], jnp.where(chip == 1, pieces[2][tail:, :], pieces[3][tail:, :]))
    last = chip == 3
    key = jnp.where(last, pieces[0][tail : tail + rows, :], own).astype(F32).T
    value = jnp.where(last, pieces[0][tail + rows :, :], own).astype(F32).T
    query_t = query.astype(F32).T
    own_score = jnp.concatenate(
        [
            jnp.sum(query_t[:, h * rows : (h + 1) * rows] * key, axis=0, keepdims=True)
            for h in range(2 * heads)
        ],
        axis=1,
    )
    stats = jnp.concatenate([top, total, own_score * SCALE] + [jnp.zeros_like(top)] * 5, axis=0)
    for n, ref in enumerate((kept_ref, sent_ref)):
        ref[:DH, :half] = mixed[:, n * half : (n + 1) * half]
        ref[:DH, half:] = value
        ref[DH:, :half] = stats[:, n * half : (n + 1) * half]
        ref[DH:, half:] = jnp.zeros((ROWSTAT, DH), F32)


def merge_kernel(seq_ref, kept_ref, got_ref, route_ref, out_ref, stat_ref, pick_ref, mask_ref):
    rows = out_ref.shape[0]
    heads = out_ref.shape[1] // DH
    half = heads * rows
    even = lax.rem(seq_ref[0], 2) == 0
    last = seq_ref[0] // 2 == 3
    has_key = even != last
    kept, got = kept_ref[DH:, :half], got_ref[DH:, :half]
    own_score = jnp.where(has_key, kept[2:3, :], got[2:3, :])
    best = jnp.maximum(jnp.maximum(kept[0:1, :], got[0:1, :]), own_score)
    factor_kept = jnp.exp(kept[0:1, :] - best)
    factor_got = jnp.exp(got[0:1, :] - best)
    factor_own = jnp.exp(own_score - best)
    total = kept[1:2, :] * factor_kept + got[1:2, :] * factor_got + factor_own
    value = jnp.where(even, got_ref[:DH, half:], kept_ref[:DH, half:])
    for h in range(heads):
        cols = slice(h * rows, (h + 1) * rows)
        part = kept_ref[:DH, cols] * factor_kept[:, cols] + got_ref[:DH, cols] * factor_got[:, cols]
        part += value * factor_own[:, cols]
        out_ref[:, h * DH : (h + 1) * DH] = part.T
    stats = [line[:, h * rows : (h + 1) * rows] for line in (best, total) for h in range(heads)]
    stats.append(jnp.zeros((DH - 2 * heads, rows), F32))
    stat_ref[...] = jnp.concatenate(stats, axis=0).T
    slots = 2 * CAP
    messages = pick_ref.shape[1] // (slots + 1)
    row, column = route_both(route_ref)
    prompt, slot = slot_of(column, ranks(row, column, rows, 1), 0, rows)
    lane = lax.broadcasted_iota(jnp.int32, (rows, slots * messages), 1)
    pick_ref[:, : slots * messages] = (lane == slot * messages + prompt).astype(F32).astype(BF)
    lane = lax.broadcasted_iota(jnp.int32, (rows, messages), 1)
    pick_ref[:, slots * messages :] = (lane == prompt).astype(F32).astype(BF)
    lane = lax.broadcasted_iota(jnp.int32, (rows, DH), 1)
    for h in range(heads):
        mask_ref[:, h * DH : (h + 1) * DH] = (lane % (slots * heads) == slot * heads + h).astype(F32)


def finish_kernel(back_ref, part_ref, stat_ref, pick_ref, mask_ref, out_ref, wide):
    heads = part_ref.shape[1] // DH
    slots = 2 * CAP
    per_message = slots * heads
    stride = MESSAGE
    messages = back_ref.shape[0] // stride
    wide[...] = back_ref[...].astype(F32)
    onehot = pick_ref[:, : slots * messages]
    chosen = pick_ref[:, slots * messages :]

    def line(at):
        return wide[pl.ds(at, messages, stride=stride), :].astype(BF)

    found = dot(chosen, line(per_message), NN)
    lane = lax.broadcasted_iota(jnp.int32, found.shape, 1)
    tops = jnp.where(lane < 3 * per_message, found, 0.0)
    totals = found - tops
    stats = stat_ref[...]
    for h in range(heads):
        cols = slice(h * DH, (h + 1) * DH)
        lines = jnp.concatenate([line(s * heads + h) for s in range(slots)], axis=0)
        got = dot(onehot, lines, NN)
        mask = mask_ref[:, cols]
        prefix_top = jnp.sum(tops * mask, axis=1, keepdims=True)
        prefix_total = jnp.sum(totals * mask, axis=1, keepdims=True)
        home_top = stats[:, h : h + 1]
        home_total = stats[:, heads + h : heads + h + 1]
        best = jnp.maximum(prefix_top, home_top)
        factor_prefix = jnp.exp(prefix_top - best) * prefix_total
        factor_home = jnp.exp(home_top - best)
        scale = 1.0 / (factor_prefix + home_total * factor_home)
        mixed = got * (factor_prefix * scale) + part_ref[:, cols] * (factor_home * scale)
        out_ref[:, cols] = mixed.astype(BF)


def body(beam_rows, route, parent, prefix_kv, pages):
    prompt_count = lax.axis_size("prompt")
    seq_count = lax.axis_size("seq")
    step_count, row_count, width = beam_rows.shape
    rows = step_count * row_count
    head_part = HQ // seq_count
    out_width = head_part * DH
    per_message = step_count * CAP * head_part
    slots = prompt_count * per_message
    seq_at = lax.axis_index("seq").astype(jnp.int32).reshape(1)
    own = beam_rows.reshape(rows, width)
    route = route.reshape(step_count, row_count)
    swap = [(i, i ^ 1) for i in range(seq_count)]

    def turn(value, k):
        return lax.ppermute(value, "seq", [(i, (i + 2 * k) % seq_count) for i in range(seq_count)])

    with jax.named_scope("rows_to_heads"):
        near = lax.ppermute(own, "seq", [(i, i + 1) for i in range(seq_count - 1)])
        far = lax.ppermute(own[:, 3 * DH :], "seq", [(4, 6), (5, 7)])
    with jax.named_scope("tokens_to_heads"):
        count = pages.shape[0] * pages.shape[1]
        pre = prefix_kv.shape[1]
        split = call(
            split_kernel,
            tuple(
                jax.ShapeDtypeStruct((2 * count + 2 * pre + (2 if k == 0 else 1) * rows, DH), BF) for k in range(4)
            ),
            ("s", seq_at), ("r", pages.reshape(count, pages.shape[2])), ("r", prefix_kv[0]), ("r", own),
            scratch=[
                pltpu.VMEM((2 * count + 2 * pre + (2 if k == 0 else 1) * rows, DH), BF) for k in range(4)
            ] + [pltpu.SemaphoreType.DMA((25,))],
            nbytes=3 << 20,
            vmem=58,
            out="r",
        )
        split = list(split)
        split[1], near = lax.optimization_barrier((split[1], near))
        split[2], split[3], far = lax.optimization_barrier((split[2], split[3], far))
        pieces = [split[0]] + [turn(split[k], k) for k in range(1, 4)]
    with jax.named_scope("slots"):
        sent, query = call(
            slots_kernel,
            (jax.ShapeDtypeStruct((slots, DH), BF), jax.ShapeDtypeStruct((rows, out_width), BF)),
            ("s", seq_at), ("v", own), ("v", near), ("v", far), ("v", route),
            scratch=[pltpu.VMEM((rows, 3 * width), BF), pltpu.VMEM((slots, DH), F32)],
            flops=2 * slots * rows * DH,
            nbytes=1 << 20,
        )
    with jax.named_scope("rows_out"):
        sent = sent.reshape(prompt_count, per_message, DH)
        arrived = lax.all_to_all(sent, "prompt", 0, 0, tiled=True).reshape(slots, DH)
    with jax.named_scope("share_cores"):
        shared = call(
            share_kernel,
            jax.ShapeDtypeStruct((KVH * 2 * pre + rows * head_part, DH), BF),
            ("v", query), *[("v", piece) for piece in pieces],
            nbytes=1 << 20,
        )
        other = lax.ppermute(shared, "seq", swap)
    with jax.named_scope("prefix_part"):
        part = call(
            prefix_kernel,
            jax.ShapeDtypeStruct((prompt_count * MESSAGE, DH), BF),
            ("v", arrived), ("v", shared), ("v", other),
            scratch=[pltpu.VMEM((prompt_count * MESSAGE, DH), F32)],
            flops=4 * slots * 1024 * DH,
            nbytes=1 << 20,
        )
    with jax.named_scope("rows_back"):
        part = part.reshape(prompt_count, MESSAGE // 2, 2, DH)
        back = lax.all_to_all(part, "prompt", 0, 0, tiled=True).reshape(-1, DH)
    with jax.named_scope("page_part"):
        payload = jax.ShapeDtypeStruct((DH + ROWSTAT, rows * head_part + DH), F32)
        kept, lent = call(
            page_kernel,
            (payload, payload),
            ("s", seq_at), ("v", shared), ("v", other), ("v", parent), *[("v", piece) for piece in pieces],
            flops=4 * rows * head_part * 4096 * DH,
            nbytes=2 << 20,
        )
        got = lax.ppermute(lent, "seq", swap)
    with jax.named_scope("page_merge"):
        merged = call(
            merge_kernel,
            (
                jax.ShapeDtypeStruct((rows, out_width), F32),
                jax.ShapeDtypeStruct((rows, DH), F32),
                jax.ShapeDtypeStruct((rows, (step_count * CAP + 1) * prompt_count), BF),
                jax.ShapeDtypeStruct((rows, out_width), F32),
            ),
            ("s", seq_at), ("v", kept), ("v", got), ("v", route),
            flops=1 << 20,
            nbytes=1 << 20,
        )
    with jax.named_scope("finish"):
        attended = call(
            finish_kernel,
            jax.ShapeDtypeStruct((rows, out_width), BF),
            ("v", back), *[("v", value) for value in merged],
            scratch=[pltpu.VMEM((prompt_count * MESSAGE, DH), F32)],
            flops=2 * slots * rows * DH,
            nbytes=1 << 20,
        )
    return attended.reshape(step_count, row_count, out_width)


def solution(mesh):
    return jax.shard_map(
        body,
        mesh=mesh,
        in_specs=(
            P(None, "prompt", "seq"),
            P(None, "prompt", None),
            P(None, "prompt"),
            P("prompt", "seq", None),
            P("prompt", "seq", None),
        ),
        out_specs=P(None, "prompt", "seq"),
        check_vma=False,
    )
```

```python
import jax
import jax.numpy as jnp
from jax import lax
from jax.experimental import pallas as pl
from jax.experimental.pallas import tpu as pltpu
from jax.sharding import PartitionSpec as P

HQ = 32
KVH = 4
DH = 128
CAP = 2
STAT = 2
ROWSTAT = 8
MESSAGE = 16 + STAT
PRE = 128
PAGE_ROWS = 512
SCALE = DH ** (-0.5)
LOG2E = 1.4426950408889634
BF = jnp.bfloat16
F32 = jnp.float32
NT = (((1,), (1,)), ((), ()))
NN = (((1,), (0,)), ((), ()))
TN = (((0,), (0,)), ((), ()))
VMEM = pl.BlockSpec(memory_space=pltpu.VMEM)
SMEM = pl.BlockSpec(memory_space=pltpu.SMEM)
HBM = pl.BlockSpec(memory_space=pltpu.HBM)


def dot(a, b, dims):
    return lax.dot_general(a, b, dims, preferred_element_type=F32)


def call(kernel, outs, *operands, scratch=(), flops=0, nbytes=0, vmem=24, out="v", name=None):
    single = not isinstance(outs, tuple)
    specs = {"v": VMEM, "s": SMEM, "r": HBM}
    result = pl.pallas_call(
        kernel,
        out_shape=(outs,) if single else outs,
        in_specs=[specs[kind] for kind, _ in operands],
        out_specs=(specs[out],) * (1 if single else len(outs)),
        scratch_shapes=list(scratch),
        compiler_params=pltpu.CompilerParams(vmem_limit_bytes=vmem << 20),
        cost_estimate=pl.CostEstimate(flops=flops, bytes_accessed=nbytes, transcendentals=0),
        name=name,
    )(*[array for _, array in operands])
    return result[0] if single else result


def split_kernel(seq_ref, pages_ref, prefix_ref, own_ref, *refs):
    count = len(refs) // 2
    out_refs, held, sems = refs[:count], refs[count:-1], refs[-1]
    chip = seq_ref[0] // 2
    core = lax.rem(seq_ref[0], 2)
    order = (1, 3, 2, 0)
    fetched = {}
    used = count
    for k in order:
        target = lax.rem(chip + k, KVH)
        pieces = [
            (ref, pl.ds(pl.multiple_of((part * KVH + target) * DH, DH), DH))
            for ref in (pages_ref, prefix_ref)
            for part in range(2)
        ]
        if k == 0:
            pieces += [(own_ref, pl.ds(0, DH)), (own_ref, pl.ds(4 * DH, DH))]
        else:
            chunk = jnp.minimum(2 - core + target, 4)
            pieces.append((own_ref, pl.ds(pl.multiple_of(chunk * DH, DH), DH)))
        at, fetched[k] = 0, []
        for source, cols in pieces:
            size = source.shape[0]
            fetched[k].append(
                pltpu.make_async_copy(source.at[:, cols], held[k].at[at : at + size, :], sems.at[used])
            )
            at += size
            used += 1
    for k in order:
        for copy in fetched[k]:
            copy.start()
    written = [pltpu.make_async_copy(held[k], out_refs[k], sems.at[k]) for k in range(count)]
    for k in order:
        for copy in fetched[k]:
            copy.wait()
        written[k].start()
    for copy in written:
        copy.wait()


def share_kernel(query_ref, *refs):
    out_ref = refs[-1]
    rows = query_ref.shape[0]
    at = 0
    for ref in refs[:-1]:
        out_ref[at : at + 2 * PRE, :] = ref[2 * PAGE_ROWS : 2 * PAGE_ROWS + 2 * PRE, :]
        at += 2 * PRE
    for h in range(query_ref.shape[1] // DH):
        out_ref[at : at + rows, :] = query_ref[:, h * DH : (h + 1) * DH]
        at += rows


def slot_of(route, rank, axis, rows):
    step = lax.broadcasted_iota(jnp.int32, route.shape, axis) >= rows // 2
    return route, step.astype(jnp.int32) * CAP + rank


def ranks(along, across, rows, axis):
    first = lax.broadcasted_iota(jnp.int32, (rows, rows), axis)
    second = lax.broadcasted_iota(jnp.int32, (rows, rows), 1 - axis)
    same = (along == across) & (first < second) & ((first < rows // 2) == (second < rows // 2))
    return jnp.sum(same.astype(jnp.int32), axis=axis, keepdims=True)


def route_both(route_ref):
    row = jnp.concatenate([route_ref[0:1, :], route_ref[1:2, :]], axis=1)
    rows = row.shape[1]
    column = jnp.broadcast_to(row, (rows, rows)).T[:, :1]
    return row, column


def slots_kernel(seq_ref, own_ref, near_ref, far_ref, route_ref, sent_ref, query_ref, line, wide):
    rows = own_ref.shape[0]
    width = own_ref.shape[1]
    heads = query_ref.shape[1] // DH
    count = sent_ref.shape[0] // heads
    line[:, 3 * DH : width] = far_ref[:, 3 * DH :]
    line[:, width : 2 * width] = near_ref[...]
    line[:, 2 * width :] = own_ref[...]
    first = pl.multiple_of((10 - seq_ref[0]) * DH, DH)
    query = line[:, pl.ds(first, query_ref.shape[1])]
    query_ref[...] = query
    row, column = route_both(route_ref)
    prompt, slot = slot_of(row, ranks(column, row, rows, 0), 1, rows)
    onehot = lax.broadcasted_iota(jnp.int32, (count, rows), 0) == prompt * (2 * CAP) + slot
    onehot = onehot.astype(F32).astype(BF)
    for h in range(heads):
        wide[pl.ds(h, count, stride=heads), :] = dot(onehot, query[:, h * DH : (h + 1) * DH], NN)
    sent_ref[...] = wide[...].astype(BF)


def thirds(value):
    high = value.astype(BF).astype(F32)
    rest = value - high
    middle = rest.astype(BF).astype(F32)
    low = (rest - middle).astype(BF).astype(F32)
    return [high, middle, low]


def prefix_kernel(query_ref, mine_ref, other_ref, out_ref, held):
    messages = out_ref.shape[0] // MESSAGE
    per_message = MESSAGE - STAT
    stats = []
    wide = 256
    blocks = [(ref, 2 * PRE * k) for ref in (mine_ref, other_ref) for k in range(KVH)]
    values_t = [ref[at + PRE : at + 2 * PRE, :].astype(F32).T.astype(BF) for ref, at in blocks]
    for c in range(query_ref.shape[0] // wide):
        query = query_ref[c * wide : (c + 1) * wide, :]
        tops, totals, parts = [], [], []
        for (ref, at), value_t in zip(blocks, values_t):
            scores = dot(ref[at : at + PRE, :], query, NT)
            top = jnp.max(scores, axis=0, keepdims=True)
            weights = jnp.exp2((scores - top) * (SCALE * LOG2E)).astype(BF)
            tops.append(top)
            totals.append(jnp.sum(weights.astype(F32), axis=0, keepdims=True))
            parts.append(dot(value_t, weights, NN))
        top = tops[0]
        for other in tops[1:]:
            top = jnp.maximum(top, other)
        total = jnp.zeros_like(top)
        mixed = jnp.zeros((DH, wide), F32)
        for block_top, block_total, block_part in zip(tops, totals, parts):
            factor = jnp.exp2((block_top - top) * (SCALE * LOG2E))
            total += block_total * factor
            mixed += block_part * factor
        top = top * SCALE
        mixed = (mixed * (1.0 / total)).T
        for i in range(wide // per_message):
            at = (c * wide // per_message + i) * MESSAGE
            held[at : at + per_message, :] = mixed[i * per_message : (i + 1) * per_message, :]
        stats += [jnp.concatenate(thirds(top) + thirds(total), axis=0)]
    stats = jnp.concatenate(stats, axis=1)
    terms = stats.shape[0]
    near_by = DH // per_message
    line = lax.broadcasted_iota(jnp.int32, (near_by, DH), 0)
    lane = lax.broadcasted_iota(jnp.int32, (near_by, DH), 1)
    mine = lane // per_message == line
    spread = jnp.concatenate(
        [
            jnp.concatenate(
                [jnp.where(mine, stats[v : v + 1, g * DH : (g + 1) * DH], 0.0) for v in range(terms)], axis=1
            )
            for g in range(messages // near_by)
        ],
        axis=0,
    ).astype(BF)
    source = lax.broadcasted_iota(jnp.int32, (terms * DH, DH), 0)
    target = lax.broadcasted_iota(jnp.int32, (terms * DH, DH), 1)
    place = (source // DH) * per_message + source % per_message
    held_stats = dot(spread, (place == target).astype(F32).astype(BF), NN)
    held[pl.ds(per_message, messages, stride=MESSAGE), :] = held_stats
    held[pl.ds(per_message + 1, messages, stride=MESSAGE), :] = jnp.zeros((messages, DH), F32)
    out_ref[...] = held[...].astype(BF)


def page_kernel(seq_ref, mine_ref, other_ref, parent_ref, *refs):
    pieces, kept_ref, sent_ref = refs[:4], refs[4], refs[5]
    first = 2 * PRE * KVH
    half = mine_ref.shape[0] - first
    rows = 2 * parent_ref.shape[1]
    heads = half // rows
    count = PAGE_ROWS
    seg = 16
    tail = 2 * count + 2 * PRE
    query = jnp.concatenate([mine_ref[first:, :], other_ref[first:, :]], axis=0)
    parent = jnp.concatenate([parent_ref[0:1, :], parent_ref[1:2, :]] * (2 * heads), axis=1)
    scores = []
    for ref in pieces:
        every = dot(ref[:count, :], query, NT)
        held = every[:seg, :]
        for j in range(1, count // seg):
            held = jnp.where(parent == j, every[j * seg : (j + 1) * seg, :], held)
        scores.append(held * SCALE)
    top = jnp.max(scores[0], axis=0, keepdims=True)
    for held in scores[1:]:
        top = jnp.maximum(top, jnp.max(held, axis=0, keepdims=True))
    total = jnp.zeros_like(top)
    mixed = jnp.zeros((DH, 2 * half), F32)
    for ref, held in zip(pieces, scores):
        weights = jnp.exp(held - top).astype(BF).astype(F32)
        total += jnp.sum(weights, axis=0, keepdims=True)
        chosen = jnp.concatenate([jnp.where(parent == j, weights, 0.0) for j in range(count // seg)], axis=0)
        mixed += dot(ref[count : 2 * count, :], chosen.astype(BF), TN)
    chip = seq_ref[0] // 2
    own = jnp.where(chip == 0, pieces[1][tail:, :], jnp.where(chip == 1, pieces[2][tail:, :], pieces[3][tail:, :]))
    last = chip == 3
    key = jnp.where(last, pieces[0][tail : tail + rows, :], own).astype(F32).T
    value = jnp.where(last, pieces[0][tail + rows :, :], own).astype(F32).T
    query_t = query.astype(F32).T
    own_score = jnp.concatenate(
        [
            jnp.sum(query_t[:, h * rows : (h + 1) * rows] * key, axis=0, keepdims=True)
            for h in range(2 * heads)
        ],
        axis=1,
    )
    stats = jnp.concatenate([top, total, own_score * SCALE] + [jnp.zeros_like(top)] * 5, axis=0)
    for n, ref in enumerate((kept_ref, sent_ref)):
        ref[:DH, :half] = mixed[:, n * half : (n + 1) * half]
        ref[:DH, half:] = value
        ref[DH:, :half] = stats[:, n * half : (n + 1) * half]
        ref[DH:, half:] = jnp.zeros((ROWSTAT, DH), F32)


def merge_kernel(seq_ref, kept_ref, got_ref, route_ref, out_ref, stat_ref, pick_ref, mask_ref):
    rows = out_ref.shape[0]
    heads = out_ref.shape[1] // DH
    half = heads * rows
    even = lax.rem(seq_ref[0], 2) == 0
    last = seq_ref[0] // 2 == 3
    has_key = even != last
    kept, got = kept_ref[DH:, :half], got_ref[DH:, :half]
    own_score = jnp.where(has_key, kept[2:3, :], got[2:3, :])
    best = jnp.maximum(jnp.maximum(kept[0:1, :], got[0:1, :]), own_score)
    factor_kept = jnp.exp(kept[0:1, :] - best)
    factor_got = jnp.exp(got[0:1, :] - best)
    factor_own = jnp.exp(own_score - best)
    total = kept[1:2, :] * factor_kept + got[1:2, :] * factor_got + factor_own
    value = jnp.where(even, got_ref[:DH, half:], kept_ref[:DH, half:])
    for h in range(heads):
        cols = slice(h * rows, (h + 1) * rows)
        part = kept_ref[:DH, cols] * factor_kept[:, cols] + got_ref[:DH, cols] * factor_got[:, cols]
        part += value * factor_own[:, cols]
        out_ref[:, h * DH : (h + 1) * DH] = part.T
    stats = [line[:, h * rows : (h + 1) * rows] for line in (best, total) for h in range(heads)]
    stats.append(jnp.zeros((DH - 2 * heads, rows), F32))
    stat_ref[...] = jnp.concatenate(stats, axis=0).T
    slots = 2 * CAP
    messages = pick_ref.shape[1] // (slots + 1)
    row, column = route_both(route_ref)
    prompt, slot = slot_of(column, ranks(row, column, rows, 1), 0, rows)
    lane = lax.broadcasted_iota(jnp.int32, (rows, slots * messages), 1)
    pick_ref[:, : slots * messages] = (lane == slot * messages + prompt).astype(F32).astype(BF)
    lane = lax.broadcasted_iota(jnp.int32, (rows, messages), 1)
    pick_ref[:, slots * messages :] = (lane == prompt).astype(F32).astype(BF)
    lane = lax.broadcasted_iota(jnp.int32, (rows, DH), 1)
    for h in range(heads):
        mask_ref[:, h * DH : (h + 1) * DH] = (lane % (slots * heads) == slot * heads + h).astype(F32)


def finish_kernel(back_ref, part_ref, stat_ref, pick_ref, mask_ref, out_ref, wide):
    heads = part_ref.shape[1] // DH
    slots = 2 * CAP
    per_message = slots * heads
    stride = MESSAGE
    messages = back_ref.shape[0] // stride
    wide[...] = back_ref[...].astype(F32)
    onehot = pick_ref[:, : slots * messages]
    chosen = pick_ref[:, slots * messages :]

    def line(at):
        return wide[pl.ds(at, messages, stride=stride), :].astype(BF)

    found = dot(chosen, line(per_message), NN)
    lane = lax.broadcasted_iota(jnp.int32, found.shape, 1)
    tops = jnp.where(lane < 3 * per_message, found, 0.0)
    totals = found - tops
    stats = stat_ref[...]
    for h in range(heads):
        cols = slice(h * DH, (h + 1) * DH)
        lines = jnp.concatenate([line(s * heads + h) for s in range(slots)], axis=0)
        got = dot(onehot, lines, NN)
        mask = mask_ref[:, cols]
        prefix_top = jnp.sum(tops * mask, axis=1, keepdims=True)
        prefix_total = jnp.sum(totals * mask, axis=1, keepdims=True)
        home_top = stats[:, h : h + 1]
        home_total = stats[:, heads + h : heads + h + 1]
        best = jnp.maximum(prefix_top, home_top)
        factor_prefix = jnp.exp(prefix_top - best) * prefix_total
        factor_home = jnp.exp(home_top - best)
        scale = 1.0 / (factor_prefix + home_total * factor_home)
        mixed = got * (factor_prefix * scale) + part_ref[:, cols] * (factor_home * scale)
        out_ref[:, cols] = mixed.astype(BF)


def body(beam_rows, route, parent, prefix_kv, pages):
    prompt_count = lax.axis_size("prompt")
    seq_count = lax.axis_size("seq")
    step_count, row_count, width = beam_rows.shape
    rows = step_count * row_count
    head_part = HQ // seq_count
    out_width = head_part * DH
    per_message = step_count * CAP * head_part
    slots = prompt_count * per_message
    seq_at = lax.axis_index("seq").astype(jnp.int32).reshape(1)
    own = beam_rows.reshape(rows, width)
    route = route.reshape(step_count, row_count)
    swap = [(i, i ^ 1) for i in range(seq_count)]

    def turn(value, k):
        return lax.ppermute(value, "seq", [(i, (i + 2 * k) % seq_count) for i in range(seq_count)])

    with jax.named_scope("rows_to_heads"):
        near = lax.ppermute(own, "seq", [(i, i + 1) for i in range(seq_count - 1)])
        far = lax.ppermute(own, "seq", [(4, 6), (5, 7)])
    with jax.named_scope("tokens_to_heads"):
        count = pages.shape[0] * pages.shape[1]
        pre = prefix_kv.shape[1]
        split = call(
            split_kernel,
            tuple(
                jax.ShapeDtypeStruct((2 * count + 2 * pre + (2 if k == 0 else 1) * rows, DH), BF) for k in range(4)
            ),
            ("s", seq_at), ("r", pages.reshape(count, pages.shape[2])), ("r", prefix_kv[0]), ("r", own),
            scratch=[
                pltpu.VMEM((2 * count + 2 * pre + (2 if k == 0 else 1) * rows, DH), BF) for k in range(4)
            ] + [pltpu.SemaphoreType.DMA((25,))],
            nbytes=3 << 20,
            vmem=58,
            out="r",
        )
        split = list(split)
        split[1], near = lax.optimization_barrier((split[1], near))
        split[2], split[3], far = lax.optimization_barrier((split[2], split[3], far))
        pieces = [split[0]] + [turn(split[k], k) for k in range(1, 4)]
    with jax.named_scope("slots"):
        sent, query = call(
            slots_kernel,
            (jax.ShapeDtypeStruct((slots, DH), BF), jax.ShapeDtypeStruct((rows, out_width), BF)),
            ("s", seq_at), ("v", own), ("v", near), ("v", far), ("v", route),
            scratch=[pltpu.VMEM((rows, 3 * width), BF), pltpu.VMEM((slots, DH), F32)],
            flops=2 * slots * rows * DH,
            nbytes=1 << 20,
        )
    with jax.named_scope("rows_out"):
        sent = sent.reshape(prompt_count, per_message, DH)
        arrived = lax.all_to_all(sent, "prompt", 0, 0, tiled=True).reshape(slots, DH)
    with jax.named_scope("share_cores"):
        shared = call(
            share_kernel,
            jax.ShapeDtypeStruct((KVH * 2 * pre + rows * head_part, DH), BF),
            ("v", query), *[("v", piece) for piece in pieces],
            nbytes=1 << 20,
        )
        other = lax.ppermute(shared, "seq", swap)
    with jax.named_scope("prefix_part"):
        part = call(
            prefix_kernel,
            jax.ShapeDtypeStruct((prompt_count * MESSAGE, DH), BF),
            ("v", arrived), ("v", shared), ("v", other),
            scratch=[pltpu.VMEM((prompt_count * MESSAGE, DH), F32)],
            flops=4 * slots * 1024 * DH,
            nbytes=1 << 20,
        )
    with jax.named_scope("rows_back"):
        part = part.reshape(prompt_count, MESSAGE // 2, 2, DH)
        back = lax.all_to_all(part, "prompt", 0, 0, tiled=True).reshape(-1, DH)
    with jax.named_scope("page_part"):
        payload = jax.ShapeDtypeStruct((DH + ROWSTAT, rows * head_part + DH), F32)
        kept, lent = call(
            page_kernel,
            (payload, payload),
            ("s", seq_at), ("v", shared), ("v", other), ("v", parent), *[("v", piece) for piece in pieces],
            flops=4 * rows * head_part * 4096 * DH,
            nbytes=2 << 20,
        )
        got = lax.ppermute(lent, "seq", swap)
    with jax.named_scope("page_merge"):
        merged = call(
            merge_kernel,
            (
                jax.ShapeDtypeStruct((rows, out_width), F32),
                jax.ShapeDtypeStruct((rows, DH), F32),
                jax.ShapeDtypeStruct((rows, (step_count * CAP + 1) * prompt_count), BF),
                jax.ShapeDtypeStruct((rows, out_width), F32),
            ),
            ("s", seq_at), ("v", kept), ("v", got), ("v", route),
            flops=1 << 20,
            nbytes=1 << 20,
        )
    with jax.named_scope("finish"):
        attended = call(
            finish_kernel,
            jax.ShapeDtypeStruct((rows, out_width), BF),
            ("v", back), *[("v", value) for value in merged],
            scratch=[pltpu.VMEM((prompt_count * MESSAGE, DH), F32)],
            flops=2 * slots * rows * DH,
            nbytes=1 << 20,
        )
    return attended.reshape(step_count, row_count, out_width)


def solution(mesh):
    return jax.shard_map(
        body,
        mesh=mesh,
        in_specs=(
            P(None, "prompt", "seq"),
            P(None, "prompt", None),
            P(None, "prompt"),
            P("prompt", "seq", None),
            P("prompt", "seq", None),
        ),
        out_specs=P(None, "prompt", "seq"),
        check_vma=False,
    )
```

```python
import jax
import jax.numpy as jnp
from jax import lax
from jax.experimental import pallas as pl
from jax.experimental.pallas import tpu as pltpu
from jax.sharding import PartitionSpec as P

HQ = 32
KVH = 4
DH = 128
CAP = 2
STAT = 2
ROWSTAT = 8
MESSAGE = 16 + STAT
PRE = 128
PAGE_ROWS = 512
SCALE = DH ** (-0.5)
LOG2E = 1.4426950408889634
BF = jnp.bfloat16
F32 = jnp.float32
NT = (((1,), (1,)), ((), ()))
NN = (((1,), (0,)), ((), ()))
TN = (((0,), (0,)), ((), ()))
VMEM = pl.BlockSpec(memory_space=pltpu.VMEM)
SMEM = pl.BlockSpec(memory_space=pltpu.SMEM)
HBM = pl.BlockSpec(memory_space=pltpu.HBM)


def dot(a, b, dims):
    return lax.dot_general(a, b, dims, preferred_element_type=F32)


def call(kernel, outs, *operands, scratch=(), flops=0, nbytes=0, vmem=24, out="v", name=None):
    single = not isinstance(outs, tuple)
    specs = {"v": VMEM, "s": SMEM, "r": HBM}
    result = pl.pallas_call(
        kernel,
        out_shape=(outs,) if single else outs,
        in_specs=[specs[kind] for kind, _ in operands],
        out_specs=(specs[out],) * (1 if single else len(outs)),
        scratch_shapes=list(scratch),
        compiler_params=pltpu.CompilerParams(vmem_limit_bytes=vmem << 20),
        cost_estimate=pl.CostEstimate(flops=flops, bytes_accessed=nbytes, transcendentals=0),
        name=name,
    )(*[array for _, array in operands])
    return result[0] if single else result


def split_kernel(seq_ref, pages_ref, prefix_ref, own_ref, *refs):
    count = len(refs) // 2
    out_refs, held, sems = refs[:count], refs[count:-1], refs[-1]
    chip = seq_ref[0] // 2
    core = lax.rem(seq_ref[0], 2)
    order = (1, 3, 2, 0)
    fetched = {}
    used = count
    for k in order:
        target = lax.rem(chip + k, KVH)
        pieces = [
            (ref, pl.ds(pl.multiple_of((part * KVH + target) * DH, DH), DH))
            for ref in (pages_ref, prefix_ref)
            for part in range(2)
        ]
        if k == 0:
            pieces += [(own_ref, pl.ds(0, DH)), (own_ref, pl.ds(4 * DH, DH))]
        else:
            chunk = jnp.minimum(2 - core + target, 4)
            pieces.append((own_ref, pl.ds(pl.multiple_of(chunk * DH, DH), DH)))
        at, fetched[k] = 0, []
        for source, cols in pieces:
            size = source.shape[0]
            fetched[k].append(
                pltpu.make_async_copy(source.at[:, cols], held[k].at[at : at + size, :], sems.at[used])
            )
            at += size
            used += 1
    for k in order:
        for copy in fetched[k]:
            copy.start()
    written = [pltpu.make_async_copy(held[k], out_refs[k], sems.at[k]) for k in range(count)]
    for k in order:
        for copy in fetched[k]:
            copy.wait()
        written[k].start()
    for copy in written:
        copy.wait()


def share_kernel(query_ref, *refs):
    out_ref = refs[-1]
    rows = query_ref.shape[0]
    at = 0
    for ref in refs[:-1]:
        out_ref[at : at + 2 * PRE, :] = ref[2 * PAGE_ROWS : 2 * PAGE_ROWS + 2 * PRE, :]
        at += 2 * PRE
    for h in range(query_ref.shape[1] // DH):
        out_ref[at : at + rows, :] = query_ref[:, h * DH : (h + 1) * DH]
        at += rows


def slot_of(route, rank, axis, rows):
    step = lax.broadcasted_iota(jnp.int32, route.shape, axis) >= rows // 2
    return route, step.astype(jnp.int32) * CAP + rank


def ranks(along, across, rows, axis):
    first = lax.broadcasted_iota(jnp.int32, (rows, rows), axis)
    second = lax.broadcasted_iota(jnp.int32, (rows, rows), 1 - axis)
    same = (along == across) & (first < second) & ((first < rows // 2) == (second < rows // 2))
    return jnp.sum(same.astype(jnp.int32), axis=axis, keepdims=True)


def route_both(route_ref):
    row = jnp.concatenate([route_ref[0:1, :], route_ref[1:2, :]], axis=1)
    rows = row.shape[1]
    column = jnp.broadcast_to(row, (rows, rows)).T[:, :1]
    return row, column


def slots_kernel(seq_ref, own_ref, near_ref, far_ref, route_ref, sent_ref, query_ref, line, wide):
    rows = own_ref.shape[0]
    width = own_ref.shape[1]
    heads = query_ref.shape[1] // DH
    count = sent_ref.shape[0] // heads
    line[:, 3 * DH : width] = far_ref[...]
    line[:, width : 2 * width] = near_ref[...]
    line[:, 2 * width :] = own_ref[...]
    first = pl.multiple_of((10 - seq_ref[0]) * DH, DH)
    query = line[:, pl.ds(first, query_ref.shape[1])]
    query_ref[...] = query
    row, column = route_both(route_ref)
    prompt, slot = slot_of(row, ranks(column, row, rows, 0), 1, rows)
    onehot = lax.broadcasted_iota(jnp.int32, (count, rows), 0) == prompt * (2 * CAP) + slot
    onehot = onehot.astype(F32).astype(BF)
    for h in range(heads):
        wide[pl.ds(h, count, stride=heads), :] = dot(onehot, query[:, h * DH : (h + 1) * DH], NN)
    sent_ref[...] = wide[...].astype(BF)


def thirds(value):
    high = value.astype(BF).astype(F32)
    rest = value - high
    middle = rest.astype(BF).astype(F32)
    low = (rest - middle).astype(BF).astype(F32)
    return [high, middle, low]


def prefix_kernel(query_ref, mine_ref, other_ref, out_ref, held):
    messages = out_ref.shape[0] // MESSAGE
    per_message = MESSAGE - STAT
    stats = []
    wide = 256
    blocks = [(ref, 2 * PRE * k) for ref in (mine_ref, other_ref) for k in range(KVH)]
    values_t = [ref[at + PRE : at + 2 * PRE, :].astype(F32).T.astype(BF) for ref, at in blocks]
    for c in range(query_ref.shape[0] // wide):
        query = query_ref[c * wide : (c + 1) * wide, :]
        tops, totals, parts = [], [], []
        for (ref, at), value_t in zip(blocks, values_t):
            scores = dot(ref[at : at + PRE, :], query, NT)
            top = jnp.max(scores, axis=0, keepdims=True)
            weights = jnp.exp2((scores - top) * (SCALE * LOG2E)).astype(BF)
            tops.append(top)
            totals.append(jnp.sum(weights.astype(F32), axis=0, keepdims=True))
            parts.append(dot(value_t, weights, NN))
        top = tops[0]
        for other in tops[1:]:
            top = jnp.maximum(top, other)
        total = jnp.zeros_like(top)
        mixed = jnp.zeros((DH, wide), F32)
        for block_top, block_total, block_part in zip(tops, totals, parts):
            factor = jnp.exp2((block_top - top) * (SCALE * LOG2E))
            total += block_total * factor
            mixed += block_part * factor
        top = top * SCALE
        mixed = (mixed * (1.0 / total)).T
        for i in range(wide // per_message):
            at = (c * wide // per_message + i) * MESSAGE
            held[at : at + per_message, :] = mixed[i * per_message : (i + 1) * per_message, :]
        stats += [jnp.concatenate(thirds(top) + thirds(total), axis=0)]
    stats = jnp.concatenate(stats, axis=1)
    terms = stats.shape[0]
    near_by = DH // per_message
    line = lax.broadcasted_iota(jnp.int32, (near_by, DH), 0)
    lane = lax.broadcasted_iota(jnp.int32, (near_by, DH), 1)
    mine = lane // per_message == line
    spread = jnp.concatenate(
        [
            jnp.concatenate(
                [jnp.where(mine, stats[v : v + 1, g * DH : (g + 1) * DH], 0.0) for v in range(terms)], axis=1
            )
            for g in range(messages // near_by)
        ],
        axis=0,
    ).astype(BF)
    source = lax.broadcasted_iota(jnp.int32, (terms * DH, DH), 0)
    target = lax.broadcasted_iota(jnp.int32, (terms * DH, DH), 1)
    place = (source // DH) * per_message + source % per_message
    held_stats = dot(spread, (place == target).astype(F32).astype(BF), NN)
    held[pl.ds(per_message, messages, stride=MESSAGE), :] = held_stats
    held[pl.ds(per_message + 1, messages, stride=MESSAGE), :] = jnp.zeros((messages, DH), F32)
    out_ref[...] = held[...].astype(BF)


def page_kernel(seq_ref, mine_ref, other_ref, parent_ref, *refs):
    pieces, kept_ref, sent_ref = refs[:4], refs[4], refs[5]
    first = 2 * PRE * KVH
    half = mine_ref.shape[0] - first
    rows = 2 * parent_ref.shape[1]
    heads = half // rows
    count = PAGE_ROWS
    seg = 16
    tail = 2 * count + 2 * PRE
    query = jnp.concatenate([mine_ref[first:, :], other_ref[first:, :]], axis=0)
    parent = jnp.concatenate([parent_ref[0:1, :], parent_ref[1:2, :]] * (2 * heads), axis=1)
    scores = []
    for ref in pieces:
        every = dot(ref[:count, :], query, NT)
        held = every[:seg, :]
        for j in range(1, count // seg):
            held = jnp.where(parent == j, every[j * seg : (j + 1) * seg, :], held)
        scores.append(held * SCALE)
    top = jnp.max(scores[0], axis=0, keepdims=True)
    for held in scores[1:]:
        top = jnp.maximum(top, jnp.max(held, axis=0, keepdims=True))
    total = jnp.zeros_like(top)
    mixed = jnp.zeros((DH, 2 * half), F32)
    for ref, held in zip(pieces, scores):
        weights = jnp.exp(held - top).astype(BF).astype(F32)
        total += jnp.sum(weights, axis=0, keepdims=True)
        chosen = jnp.concatenate([jnp.where(parent == j, weights, 0.0) for j in range(count // seg)], axis=0)
        mixed += dot(ref[count : 2 * count, :], chosen.astype(BF), TN)
    chip = seq_ref[0] // 2
    own = jnp.where(chip == 0, pieces[1][tail:, :], jnp.where(chip == 1, pieces[2][tail:, :], pieces[3][tail:, :]))
    last = chip == 3
    key = jnp.where(last, pieces[0][tail : tail + rows, :], own).astype(F32).T
    value = jnp.where(last, pieces[0][tail + rows :, :], own).astype(F32).T
    query_t = query.astype(F32).T
    own_score = jnp.concatenate(
        [
            jnp.sum(query_t[:, h * rows : (h + 1) * rows] * key, axis=0, keepdims=True)
            for h in range(2 * heads)
        ],
        axis=1,
    )
    stats = jnp.concatenate([top, total, own_score * SCALE] + [jnp.zeros_like(top)] * 5, axis=0)
    for n, ref in enumerate((kept_ref, sent_ref)):
        ref[:DH, :half] = mixed[:, n * half : (n + 1) * half]
        ref[:DH, half:] = value
        ref[DH:, :half] = stats[:, n * half : (n + 1) * half]
        ref[DH:, half:] = jnp.zeros((ROWSTAT, DH), F32)


def merge_kernel(seq_ref, kept_ref, got_ref, route_ref, out_ref, stat_ref, pick_ref, mask_ref):
    rows = out_ref.shape[0]
    heads = out_ref.shape[1] // DH
    half = heads * rows
    even = lax.rem(seq_ref[0], 2) == 0
    last = seq_ref[0] // 2 == 3
    has_key = even != last
    kept, got = kept_ref[DH:, :half], got_ref[DH:, :half]
    own_score = jnp.where(has_key, kept[2:3, :], got[2:3, :])
    best = jnp.maximum(jnp.maximum(kept[0:1, :], got[0:1, :]), own_score)
    factor_kept = jnp.exp(kept[0:1, :] - best)
    factor_got = jnp.exp(got[0:1, :] - best)
    factor_own = jnp.exp(own_score - best)
    total = kept[1:2, :] * factor_kept + got[1:2, :] * factor_got + factor_own
    value = jnp.where(even, got_ref[:DH, half:], kept_ref[:DH, half:])
    for h in range(heads):
        cols = slice(h * rows, (h + 1) * rows)
        part = kept_ref[:DH, cols] * factor_kept[:, cols] + got_ref[:DH, cols] * factor_got[:, cols]
        part += value * factor_own[:, cols]
        out_ref[:, h * DH : (h + 1) * DH] = part.T
    stats = [line[:, h * rows : (h + 1) * rows] for line in (best, total) for h in range(heads)]
    stats.append(jnp.zeros((DH - 2 * heads, rows), F32))
    stat_ref[...] = jnp.concatenate(stats, axis=0).T
    slots = 2 * CAP
    messages = pick_ref.shape[1] // (slots + 1)
    row, column = route_both(route_ref)
    prompt, slot = slot_of(column, ranks(row, column, rows, 1), 0, rows)
    lane = lax.broadcasted_iota(jnp.int32, (rows, slots * messages), 1)
    pick_ref[:, : slots * messages] = (lane == slot * messages + prompt).astype(F32).astype(BF)
    lane = lax.broadcasted_iota(jnp.int32, (rows, messages), 1)
    pick_ref[:, slots * messages :] = (lane == prompt).astype(F32).astype(BF)
    lane = lax.broadcasted_iota(jnp.int32, (rows, DH), 1)
    for h in range(heads):
        mask_ref[:, h * DH : (h + 1) * DH] = (lane % (slots * heads) == slot * heads + h).astype(F32)


def finish_kernel(back_ref, part_ref, stat_ref, pick_ref, mask_ref, out_ref, wide):
    heads = part_ref.shape[1] // DH
    slots = 2 * CAP
    per_message = slots * heads
    stride = MESSAGE
    messages = back_ref.shape[0] // stride
    wide[...] = back_ref[...].astype(F32)
    onehot = pick_ref[:, : slots * messages]
    chosen = pick_ref[:, slots * messages :]

    def line(at):
        return wide[pl.ds(at, messages, stride=stride), :].astype(BF)

    found = dot(chosen, line(per_message), NN)
    lane = lax.broadcasted_iota(jnp.int32, found.shape, 1)
    tops = jnp.where(lane < 3 * per_message, found, 0.0)
    totals = found - tops
    stats = stat_ref[...]
    for h in range(heads):
        cols = slice(h * DH, (h + 1) * DH)
        lines = jnp.concatenate([line(s * heads + h) for s in range(slots)], axis=0)
        got = dot(onehot, lines, NN)
        mask = mask_ref[:, cols]
        prefix_top = jnp.sum(tops * mask, axis=1, keepdims=True)
        prefix_total = jnp.sum(totals * mask, axis=1, keepdims=True)
        home_top = stats[:, h : h + 1]
        home_total = stats[:, heads + h : heads + h + 1]
        best = jnp.maximum(prefix_top, home_top)
        factor_prefix = jnp.exp(prefix_top - best) * prefix_total
        factor_home = jnp.exp(home_top - best)
        scale = 1.0 / (factor_prefix + home_total * factor_home)
        mixed = got * (factor_prefix * scale) + part_ref[:, cols] * (factor_home * scale)
        out_ref[:, cols] = mixed.astype(BF)


def body(beam_rows, route, parent, prefix_kv, pages):
    prompt_count = lax.axis_size("prompt")
    seq_count = lax.axis_size("seq")
    step_count, row_count, width = beam_rows.shape
    rows = step_count * row_count
    head_part = HQ // seq_count
    out_width = head_part * DH
    per_message = step_count * CAP * head_part
    slots = prompt_count * per_message
    seq_at = lax.axis_index("seq").astype(jnp.int32).reshape(1)
    own = beam_rows.reshape(rows, width)
    route = route.reshape(step_count, row_count)
    swap = [(i, i ^ 1) for i in range(seq_count)]

    def turn(value, k):
        return lax.ppermute(value, "seq", [(i, (i + 2 * k) % seq_count) for i in range(seq_count)])

    with jax.named_scope("rows_to_heads"):
        near = lax.ppermute(own, "seq", [(i, i + 1) for i in range(seq_count - 1)])
        far = lax.ppermute(own[:, 3 * DH :], "seq", [(4, 6), (5, 7)])
    with jax.named_scope("tokens_to_heads"):
        count = pages.shape[0] * pages.shape[1]
        pre = prefix_kv.shape[1]
        split = call(
            split_kernel,
            tuple(
                jax.ShapeDtypeStruct((2 * count + 2 * pre + (2 if k == 0 else 1) * rows, DH), BF) for k in range(4)
            ),
            ("s", seq_at), ("r", pages.reshape(count, pages.shape[2])), ("r", prefix_kv[0]), ("r", own),
            scratch=[
                pltpu.VMEM((2 * count + 2 * pre + (2 if k == 0 else 1) * rows, DH), BF) for k in range(4)
            ] + [pltpu.SemaphoreType.DMA((25,))],
            nbytes=3 << 20,
            vmem=58,
            out="r",
        )
        split = list(split)
        split[3], near = lax.optimization_barrier((split[3], near))
        split[2], split[1], far = lax.optimization_barrier((split[2], split[1], far))
        pieces = [split[0]] + [turn(split[k], k) for k in range(1, 4)]
    with jax.named_scope("slots"):
        sent, query = call(
            slots_kernel,
            (jax.ShapeDtypeStruct((slots, DH), BF), jax.ShapeDtypeStruct((rows, out_width), BF)),
            ("s", seq_at), ("v", own), ("v", near), ("v", far), ("v", route),
            scratch=[pltpu.VMEM((rows, 3 * width), BF), pltpu.VMEM((slots, DH), F32)],
            flops=2 * slots * rows * DH,
            nbytes=1 << 20,
        )
    with jax.named_scope("rows_out"):
        sent = sent.reshape(prompt_count, per_message, DH)
        arrived = lax.all_to_all(sent, "prompt", 0, 0, tiled=True).reshape(slots, DH)
    with jax.named_scope("share_cores"):
        shared = call(
            share_kernel,
            jax.ShapeDtypeStruct((KVH * 2 * pre + rows * head_part, DH), BF),
            ("v", query), *[("v", piece) for piece in pieces],
            nbytes=1 << 20,
        )
        other = lax.ppermute(shared, "seq", swap)
    with jax.named_scope("prefix_part"):
        part = call(
            prefix_kernel,
            jax.ShapeDtypeStruct((prompt_count * MESSAGE, DH), BF),
            ("v", arrived), ("v", shared), ("v", other),
            scratch=[pltpu.VMEM((prompt_count * MESSAGE, DH), F32)],
            flops=4 * slots * 1024 * DH,
            nbytes=1 << 20,
        )
    with jax.named_scope("rows_back"):
        part = part.reshape(prompt_count, MESSAGE // 2, 2, DH)
        back = lax.all_to_all(part, "prompt", 0, 0, tiled=True).reshape(-1, DH)
    with jax.named_scope("page_part"):
        payload = jax.ShapeDtypeStruct((DH + ROWSTAT, rows * head_part + DH), F32)
        kept, lent = call(
            page_kernel,
            (payload, payload),
            ("s", seq_at), ("v", shared), ("v", other), ("v", parent), *[("v", piece) for piece in pieces],
            flops=4 * rows * head_part * 4096 * DH,
            nbytes=2 << 20,
        )
        got = lax.ppermute(lent, "seq", swap)
    with jax.named_scope("page_merge"):
        merged = call(
            merge_kernel,
            (
                jax.ShapeDtypeStruct((rows, out_width), F32),
                jax.ShapeDtypeStruct((rows, DH), F32),
                jax.ShapeDtypeStruct((rows, (step_count * CAP + 1) * prompt_count), BF),
                jax.ShapeDtypeStruct((rows, out_width), F32),
            ),
            ("s", seq_at), ("v", kept), ("v", got), ("v", route),
            flops=1 << 20,
            nbytes=1 << 20,
        )
    with jax.named_scope("finish"):
        attended = call(
            finish_kernel,
            jax.ShapeDtypeStruct((rows, out_width), BF),
            ("v", back), *[("v", value) for value in merged],
            scratch=[pltpu.VMEM((prompt_count * MESSAGE, DH), F32)],
            flops=2 * slots * rows * DH,
            nbytes=1 << 20,
        )
    return attended.reshape(step_count, row_count, out_width)


def solution(mesh):
    return jax.shard_map(
        body,
        mesh=mesh,
        in_specs=(
            P(None, "prompt", "seq"),
            P(None, "prompt", None),
            P(None, "prompt"),
            P("prompt", "seq", None),
            P("prompt", "seq", None),
        ),
        out_specs=P(None, "prompt", "seq"),
        check_vma=False,
    )
```
